512 devices in a mesh: blk: 64 (over x, z, core), rhs: 8 (over y).
Axes of the slice: x: 4, y: 8, z: 8, core: 2. Of those that a mesh axis runs over, the one named last changes fastest.
Arguments:
- rhs_vectors: float32 [64, 131072], P('rhs', 'blk'), may hold values from -6 to 6
- diag_inverse: float32 [2, 512, 256, 256], P(None, 'blk', 'rhs'), as said below
- near_left: float32 [2, 1792, 32, 256], P(None, 'blk'), may hold values from -0.375 to 0.375
- near_right: float32 [2, 1792, 32, 256], P(None, 'blk'), may hold values from -0.375 to 0.375
- near_rank: int32 [2, 1792], P(None, 'blk'), may hold values from 8 to 32
- near_pattern: int32 [2, 1792], P(None, 'blk'), may hold values 0 or 1
- far_row: float32 [2, 512, 32, 256], P(None, 'blk'), may hold values from -0.0625 to 0.0625
- far_col: float32 [2, 512, 32, 256], P(None, 'blk'), may hold values from -0.0625 to 0.0625
Outputs:
- solution: float32 [64, 131072], P('rhs', 'blk')
The draws below stay inside these ranges and needn't reach their ends.
Inputs may be any that keep to these rules, and one draw needn't show every extreme that they name: Each tile within a group uses only its first near_rank factor rows. A tile within a group with near_pattern 0 is absent. `diag_inverse`: each block is a positive diagonal plus small entries off it.
All inputs are finite; a program needn't handle non-finite values.
Results may differ from the reference program's by a relative error of at most 0.0003.
Values sent between devices are 32-bit elements; how exact they have to be, the bound alone decides.
A program may use at most 64 MiB of HBM per device.

```python
import math
import jax
import jax.numpy as jnp
from jax import lax

B = 256
RK = 32
BPD = 8
NRHS = 64
NB = 512
ORDER = 131072
NP = 28
NPAIRS = 1792
N_BLK = 64


def draw_diag_inverse(key, part):
    key_diag, key_off = jax.random.split(jax.random.fold_in(key, 11))
    shape = (2, NB, B, B)
    off_diag = jax.random.normal(key_off, shape, jnp.float32) * (0.5 / math.sqrt(B))
    diag_values = jax.random.uniform(key_diag, (2, NB, B), jnp.float32, 0.5, 1.5)
    identity = jnp.eye(B, dtype=jnp.float32)
    return off_diag * (1.0 - identity) + identity * diag_values[..., None]


def place_ends(array, key, low, largest):
    shape = array.shape
    place = [jax.random.randint(jax.random.fold_in(key, axis), (), 0, shape[axis]) for axis in range(len(shape))]
    array = array.at[tuple(place)].set(low)
    longest = shape.index(max(shape))
    place[longest] = (place[longest] + 1) % shape[longest]
    return array.at[tuple(place)].set(largest)


def levels(rng, shape, cuts, low, high):
    def one(dim, parts):
        steps = jax.random.uniform(jax.random.fold_in(jax.random.fold_in(rng, 6), dim), (parts,), jnp.float32, low / len(cuts), high / len(cuts))
        return jnp.repeat(jnp.exp(steps), shape[dim] // parts).reshape((-1,) + (1,) * (len(shape) - dim - 1))

    level = one(*cuts[0])
    for cut in cuts[1:]:
        level = level * one(*cut)
    return level


def gaussian(rng, dims, scale, bound, shards=(), kind=jnp.bfloat16):
    factor_of = levels(rng, dims, shards, -0.22, 0.18) if shards else 1.0
    array = jax.random.normal(rng, dims, jnp.float32) * scale * factor_of
    return jnp.minimum(jnp.maximum(array, -bound), bound).astype(kind)


def setup_inputs(seed: int = 0) -> dict:
    key_of = jax.random.split(jax.random.key(seed), 9)
    rhs_vectors = gaussian(key_of[0], (NRHS, ORDER), 1.0, 6.0, ((0, 8), (1, 64)), jnp.float32)
    diag_inverse = draw_diag_inverse(jax.random.fold_in(key_of[8], 71), 0)
    near_left = gaussian(key_of[2], (2, NPAIRS, RK, B), B ** -0.5, 0.375, ((1, 64),), jnp.float32)
    near_right = gaussian(key_of[3], (2, NPAIRS, RK, B), B ** -0.5, 0.375, ((1, 64),), jnp.float32)
    near_rank = place_ends(jax.random.randint(key_of[4], (2, NPAIRS), RK // 4, RK + 1), jax.random.fold_in(key_of[4], 1), RK // 4, RK).astype(jnp.int32)
    near_pattern = place_ends((jax.random.randint(key_of[5], (2, NPAIRS), 0, 4) < 3).astype(jnp.int32), jax.random.fold_in(key_of[5], 1), 0, 1)
    far_row = gaussian(key_of[6], (2, NB, RK, B), (B * RK) ** -0.5, 0.0625, ((1, 64),), jnp.float32)
    far_col = gaussian(key_of[7], (2, NB, RK, B), (B * RK) ** -0.5, 0.0625, ((1, 64),), jnp.float32)
    return {"rhs_vectors": rhs_vectors, "diag_inverse": diag_inverse, "near_left": near_left, "near_right": near_right, "near_rank": near_rank, "near_pattern": near_pattern, "far_row": far_row, "far_col": far_col}


HIGHEST = lax.Precision.HIGHEST


def times_high(first, second):
    return jnp.dot(first, second, precision=HIGHEST, preferred_element_type=jnp.float32)


def times_trans(first, second):
    return lax.dot_general(first, second, (((1,), (1,)), ((), ())), precision=HIGHEST, preferred_element_type=jnp.float32)


def pair_index(higher, lower):
    return higher * (higher - 1) // 2 + lower


def group_sweep(side_list, carried, inverse, left_tiles, right_tiles, keep_mask, row_gen, block_order):
    solved = {}
    finished = []
    for target in block_order:
        current = side_list[target] - times_high(carried, row_gen[target])
        for source in finished:
            pair_slot = pair_index(max(target, source), min(target, source))
            reduced = times_trans(solved[source], right_tiles[pair_slot]) * keep_mask[pair_slot]
            current = current - times_high(reduced, left_tiles[pair_slot])
        solved[target] = times_trans(current, inverse[target])
        finished.append(target)
    return [solved[target] for target in range(len(side_list))]


def make_step(block_order):
    def step_fn(carried, pieces):
        side_arr, inv_arr, left_arr, right_arr, keep_arr, row_arr, col_arr = pieces
        solved = group_sweep([side_arr[t] for t in range(BPD)], carried, inv_arr, left_arr, right_arr, keep_arr, row_arr, block_order)
        updated = carried
        for target in range(BPD):
            updated = updated + times_trans(solved[target], col_arr[target])
        return updated, jnp.stack(solved)
    return step_fn


def reference(rhs_vectors, diag_inverse, near_left, near_right, near_rank, near_pattern, far_row, far_col):
    row_count = rhs_vectors.shape[0]
    sides = rhs_vectors.reshape(row_count, N_BLK, BPD, B).transpose(1, 2, 0, 3)
    inverse = diag_inverse.reshape(2, N_BLK, BPD, B, B)
    left_tiles = near_left.reshape(2, N_BLK, NP, RK, B)
    right_tiles = near_right.reshape(2, N_BLK, NP, RK, B)
    columns = jnp.arange(RK, dtype=jnp.int32)
    rank_grid = near_rank.reshape(2, N_BLK, NP)[..., None]
    pattern_grid = near_pattern.reshape(2, N_BLK, NP)[..., None]
    keep_mask = jnp.where((columns < rank_grid) & (pattern_grid == 1), 1.0, 0.0).astype(jnp.float32)
    row_gen = far_row.reshape(2, N_BLK, BPD, RK, B)
    col_gen = far_col.reshape(2, N_BLK, BPD, RK, B)
    initial = jnp.zeros((row_count, RK), jnp.float32)
    lower_pieces = (sides, inverse[0], left_tiles[0], right_tiles[0], keep_mask[0], row_gen[0], col_gen[0])
    _, lower_out = lax.scan(make_step(list(range(BPD))), initial, lower_pieces)
    upper_pieces = (lower_out, inverse[1], left_tiles[1], right_tiles[1], keep_mask[1], row_gen[1], col_gen[1])
    _, upper_out = lax.scan(make_step(list(range(BPD - 1, -1, -1))), initial, upper_pieces, reverse=True)
    return upper_out.transpose(2, 0, 1, 3).reshape(row_count, ORDER)
```

```python
import functools

import jax
import jax.numpy as jnp
from jax import lax
from jax.experimental import pallas as pl
from jax.experimental.pallas import tpu as pltpu
from jax.sharding import PartitionSpec as P

F32 = jnp.float32
BF16 = jnp.bfloat16
MESH = pl.DeviceIdType.MESH

WIDTH = 256
RANK = 32
BLOCKS = 8
RING = 8
SHARE = WIDTH // RING
SLAB = 16
SLABS = 4
UNITS = 2 * BLOCKS
SLACK = 2
LANES = 128
PACK = LANES // RANK

ORDER = [(0, m) for m in range(BLOCKS)] + [(1, m) for m in reversed(range(BLOCKS))]


def pair_index(a, b):
    high, low = max(a, b), min(a, b)
    return high * (high - 1) // 2 + low


def hop_count(unit, side):
    return 4 if (unit + side) % 2 == 0 else 3


def parts(x):
    high = x.astype(BF16)
    return high, (x - high.astype(F32)).astype(BF16)


def times(a, b, trans):
    rows = a.shape[0]
    top = a.astype(BF16).astype(F32)
    stacked = jnp.concatenate([top, a - top], axis=0).astype(BF16)
    dims = (((1,), (1 if trans else 0,)), ((), ()))
    high, low = parts(b)
    p = lax.dot_general(stacked, high, dims, preferred_element_type=F32)
    q = lax.dot_general(stacked, low, dims, preferred_element_type=F32)
    p = p + q
    return p[:rows] + p[rows:]


def kernel(
    rhs_hbm, diag_hbm, left_hbm, right_hbm, rank_ref, pattern_ref, row_hbm, col_hbm,
    out_ref,
    rhs, inv, left, right, row, col, sol0, sol1, red, pack, xpack,
    load_sem, own_sem, ring_send, ring_recv, slab_send, slab_recv, x_send, x_recv,
):
    g = lax.axis_index("blk")
    y = lax.axis_index("rhs")
    slab, place = g // SLAB, g % SLAB

    loads = [[], []]
    loads[0].append(pltpu.make_async_copy(rhs_hbm, rhs, load_sem.at[8]))
    for s in range(2):
        for i, (src, dst) in enumerate(
            ((row_hbm, row), (col_hbm, col), (left_hbm, left), (right_hbm, right))
        ):
            loads[s].append(pltpu.make_async_copy(src.at[s], dst.at[s], load_sem.at[4 * s + i]))
    mine = pl.ds(SHARE * y, SHARE)
    own = [
        pltpu.make_async_copy(diag_hbm.at[s], inv.at[s, :, mine, :], own_sem.at[s]) for s in range(2)
    ]
    for s in range(2):
        for c in loads[s]:
            c.start()
        own[s].start()

    barrier = pltpu.get_barrier_semaphore()
    ring = ((y + 1) % RING, (y + RING - 1) % RING)
    for n in ring:
        pl.semaphore_signal(barrier, inc=1, device_id=(g, n), device_id_type=MESH)
    for d in range(1, SLAB):
        pl.semaphore_signal(
            barrier, inc=1, device_id=(slab * SLAB + (place + d) % SLAB, y), device_id_type=MESH
        )
    for d in range(1, SLABS):
        pl.semaphore_signal(
            barrier, inc=1, device_id=(((slab + d) % SLABS) * SLAB + place, y), device_id_type=MESH
        )
    pl.semaphore_wait(barrier, 2 + SLAB - 1 + SLABS - 1)

    def shard(unit, origin):
        s, m = ORDER[unit]
        return inv.at[s, m, pl.ds(SHARE * origin, SHARE), :]

    def origin_of(side, hop):
        return (y + RING - hop) % RING if side == 0 else (y + hop) % RING

    def ring_copy(unit, side, hop):
        s, m = ORDER[unit]
        there = shard(unit, origin_of(side, hop - 1) if hop > 1 else y)
        return pltpu.make_async_remote_copy(
            src_ref=diag_hbm.at[s, m] if hop == 1 else there,
            dst_ref=there,
            send_sem=ring_send.at[unit, side, hop - 1],
            recv_sem=ring_recv.at[unit, side, hop - 1],
            device_id=(g, ring[side]),
            device_id_type=MESH,
        )

    def ring_arrived(unit, side, hop):
        here = shard(unit, origin_of(side, hop))
        pltpu.make_async_remote_copy(
            src_ref=here,
            dst_ref=here,
            send_sem=ring_send.at[unit, side, hop - 1],
            recv_sem=ring_recv.at[unit, side, hop - 1],
            device_id=(g, ring[side]),
            device_id_type=MESH,
        ).wait_recv()

    lane = lax.broadcasted_iota(jnp.int32, (8, WIDTH), 1)
    slot_of, within = lane // RANK, lane % RANK
    lane128 = lax.broadcasted_iota(jnp.int32, (8, LANES), 1)
    sub128 = lax.broadcasted_iota(jnp.int32, (8, LANES), 0)
    totals = [jnp.zeros((40, LANES), F32), jnp.zeros((72, LANES), F32)]

    def solve(unit):
        s, m = ORDER[unit]
        rows = 40 if s == 0 else 72
        earlier = list(range(m)) if s == 0 else list(range(m + 1, BLOCKS))
        later = list(range(m + 1, BLOCKS)) if s == 0 else list(range(m))
        if s == 0:
            side = jnp.concatenate([rhs[:, m * WIDTH : (m + 1) * WIDTH], -row[0, m]], axis=0)
        else:
            side = jnp.concatenate([sol0[m], -row[1, m]], axis=0)
        if earlier:
            ranks = jnp.zeros((8, WIDTH), jnp.int32)
            reduced = jnp.zeros((rows, WIDTH), F32)
            for k in earlier:
                p = pair_index(m, k)
                rank = jnp.where(pattern_ref[s, p] == 1, rank_ref[s, p], 0)
                ranks = jnp.where(slot_of == (m ^ k), rank, ranks)
                hit = jnp.tile(slot_of == (m ^ k), (rows // 8, 1))
                reduced = jnp.where(hit, red[k, :rows, :], reduced)
            keep = jnp.where(within < ranks, 1.0, 0.0).astype(F32)
            reduced = reduced * jnp.tile(keep, (rows // 8, 1))
            tiles = [
                left[s, pair_index(m, m ^ j)] if (m ^ j) in earlier else jnp.zeros((RANK, WIDTH), F32)
                for j in range(BLOCKS)
            ]
            side = side - times(reduced, jnp.concatenate(tiles, axis=0), False)
        solved = times(side, inv[s, m], True)
        if s == 0:
            sol0[m] = solved
        else:
            sol1[m] = solved
        tiles = [col[s, m]] + [
            right[s, pair_index(m, m ^ j)] if (m ^ j) in later else jnp.zeros((RANK, WIDTH), F32)
            for j in range(1, BLOCKS)
        ]
        if later:
            after = times(solved, jnp.concatenate(tiles, axis=0), True)
            red[m, :rows, :] = after
            totals[s] = totals[s] + after[:, :LANES]
        else:
            after = times(solved, jnp.concatenate(tiles[:PACK], axis=0), True)
            totals[s] = totals[s] + after

    low_lanes = lane128 < RANK
    unit_pack = jnp.concatenate(
        [
            jnp.where(lane128 % RANK == sub128 + 8 * (lane128 // RANK), 1.0, 0.0).astype(F32),
            jnp.zeros((8, LANES), F32),
        ],
        axis=0,
    )

    def packed(gain_rows, v):
        a = unit_pack[:8]
        for i in range(PACK):
            piece = jnp.where(low_lanes, gain_rows[8 * i : 8 * i + 8], 0.0)
            a = a + (pltpu.roll(piece, RANK * i, 1) if i else piece)
        return jnp.concatenate([a, jnp.where(low_lanes, v, 0.0)], axis=0)

    def spread(m):
        a = m[:8]
        rolled = [a if i == 0 else pltpu.roll(a, RANK * i, 1) for i in range(PACK)]
        strips = []
        for b in range(PACK):
            for i in range(PACK):
                strips.append(jnp.where(lane128 // RANK == b, rolled[(b - i) % PACK], 0.0))
        return jnp.concatenate(strips, axis=0)

    only_v = jnp.concatenate([jnp.zeros((8, LANES), F32), jnp.ones((8, LANES), F32)], axis=0)

    def after(first, then):
        return times(first, spread(then), False) + then * only_v

    def product(maps):
        while len(maps) > 1:
            maps = [after(maps[i], maps[i + 1]) for i in range(0, len(maps), 2)]
        return maps[0]

    def slab_copy(s, d):
        return pltpu.make_async_remote_copy(
            src_ref=pack.at[s, place],
            dst_ref=pack.at[s, place],
            send_sem=slab_send.at[s, d - 1],
            recv_sem=slab_recv.at[s, d - 1],
            device_id=(slab * SLAB + (place + d) % SLAB, y),
            device_id_type=MESH,
        )

    def slab_arrived(s, d):
        here = pack.at[s, (place + SLAB - d) % SLAB]
        pltpu.make_async_remote_copy(
            src_ref=here,
            dst_ref=here,
            send_sem=slab_send.at[s, d - 1],
            recv_sem=slab_recv.at[s, d - 1],
            device_id=(slab * SLAB + (place + d) % SLAB, y),
            device_id_type=MESH,
        ).wait_recv()

    def x_copy(s, d):
        return pltpu.make_async_remote_copy(
            src_ref=xpack.at[s, slab],
            dst_ref=xpack.at[s, slab],
            send_sem=x_send.at[s, d - 1],
            recv_sem=x_recv.at[s, d - 1],
            device_id=(((slab + d) % SLABS) * SLAB + place, y),
            device_id_type=MESH,
        )

    def x_arrived(s, d):
        here = xpack.at[s, (slab + SLABS - d) % SLABS]
        pltpu.make_async_remote_copy(
            src_ref=here,
            dst_ref=here,
            send_sem=x_send.at[s, d - 1],
            recv_sem=x_recv.at[s, d - 1],
            device_id=(((slab + d) % SLABS) * SLAB + place, y),
            device_id_type=MESH,
        ).wait_recv()

    def exchange_start(s, packet):
        pack[s, place] = packet
        for d in range(1, SLAB):
            slab_copy(s, d).start()

    def exchange_middle(s):
        for d in range(1, SLAB):
            slab_arrived(s, d)
        order = list(range(SLAB)) if s == 0 else list(reversed(range(SLAB)))
        maps = [pack[s, i] for i in order]
        whole = product(maps)
        xpack[s, slab] = whole
        for d in range(1, SLABS):
            x_copy(s, d).start()
        ahead = [
            jnp.where((place > i) if s == 0 else (place < i), one, unit_pack)
            for i, one in zip(order, maps)
        ]
        return product(ahead)

    def exchange_end(s, ahead):
        for d in range(1, SLABS):
            x_arrived(s, d)
        order = list(range(SLABS)) if s == 0 else list(reversed(range(SLABS)))
        maps = [
            jnp.where((slab > i) if s == 0 else (slab < i), xpack[s, i], unit_pack) for i in order
        ]
        entering = product([product(maps), ahead])
        return entering[8:]

    lower_ready = {}
    span = 4 * SLACK
    carried = None
    for tick in range(UNITS + span):
        for hop in (4, 3, 2, 1):
            unit = tick - SLACK * (hop - 1)
            if not 0 <= unit < UNITS:
                continue
            for side in range(2):
                if hop > hop_count(unit, side):
                    continue
                if hop > 1:
                    ring_arrived(unit, side, hop - 1)
                ring_copy(unit, side, hop).start()
        unit = tick - span
        if unit < 0:
            continue
        if unit == 0:
            for c in loads[0]:
                c.wait()
            own[0].wait()
        if unit == BLOCKS:
            for c in loads[1]:
                c.wait()
            own[1].wait()
        for side in range(2):
            ring_arrived(unit, side, hop_count(unit, side))
        solve(unit)
        if unit == BLOCKS - 1:
            exchange_start(0, packed(totals[0][8:40], totals[0][:8]))
        if unit == BLOCKS + 2:
            lower_ready["ahead"] = exchange_middle(0)
        if unit == BLOCKS + 5:
            carried = exchange_end(0, lower_ready["ahead"])

    upper_v = totals[1][:8] + times(carried[:, :RANK], totals[1][8:40], False)
    exchange_start(1, packed(totals[1][40:72], upper_v))
    entering = exchange_end(1, exchange_middle(1))

    both = carried + pltpu.roll(entering, RANK, 1)
    for m in range(BLOCKS):
        out_ref[:, m * WIDTH : (m + 1) * WIDTH] = sol1[m, 0:8, :] + times(
            both[:, : 2 * RANK], sol1[m, 8:72, :], False
        )

    for unit in range(UNITS):
        for side in range(2):
            for hop in range(1, hop_count(unit, side) + 1):
                ring_copy(unit, side, hop).wait_send()
    for s in range(2):
        for d in range(1, SLAB):
            slab_copy(s, d).wait_send()
        for d in range(1, SLABS):
            x_copy(s, d).wait_send()


def shards(rhs, diag, left, right, rank, pattern, row, col):
    hbm = pl.BlockSpec(memory_space=pl.ANY)
    smem = pl.BlockSpec(memory_space=pltpu.SMEM)
    return pl.pallas_call(
        kernel,
        out_shape=jax.ShapeDtypeStruct(rhs.shape, F32),
        in_specs=[hbm, hbm, hbm, hbm, smem, smem, hbm, hbm],
        out_specs=pl.BlockSpec(memory_space=pltpu.VMEM),
        scratch_shapes=[
            pltpu.VMEM(rhs.shape, F32),
            pltpu.VMEM((2, BLOCKS, WIDTH, WIDTH), F32),
            pltpu.VMEM(left.shape, F32),
            pltpu.VMEM(right.shape, F32),
            pltpu.VMEM(row.shape, F32),
            pltpu.VMEM(col.shape, F32),
            pltpu.VMEM((BLOCKS, 40, WIDTH), F32),
            pltpu.VMEM((BLOCKS, 72, WIDTH), F32),
            pltpu.VMEM((BLOCKS, 72, WIDTH), F32),
            pltpu.VMEM((2, SLAB, 16, LANES), F32),
            pltpu.VMEM((2, SLABS, 16, LANES), F32),
            pltpu.SemaphoreType.DMA((9,)),
            pltpu.SemaphoreType.DMA((2,)),
            pltpu.SemaphoreType.DMA((UNITS, 2, 4)),
            pltpu.SemaphoreType.DMA((UNITS, 2, 4)),
            pltpu.SemaphoreType.DMA((2, SLAB - 1)),
            pltpu.SemaphoreType.DMA((2, SLAB - 1)),
            pltpu.SemaphoreType.DMA((2, SLABS - 1)),
            pltpu.SemaphoreType.DMA((2, SLABS - 1)),
        ],
        compiler_params=pltpu.CompilerParams(
            collective_id=0, has_side_effects=True, vmem_limit_bytes=40 * 1024 * 1024
        ),
        cost_estimate=pl.CostEstimate(
            flops=400_000_000, bytes_accessed=6_000_000, transcendentals=0
        ),
    )(rhs, diag, left, right, rank, pattern, row, col)


def solution(mesh):
    return jax.shard_map(
        shards,
        mesh=mesh,
        in_specs=(
            P("rhs", "blk"),
            P(None, "blk", "rhs", None),
            P(None, "blk", None, None),
            P(None, "blk", None, None),
            P(None, "blk"),
            P(None, "blk"),
            P(None, "blk", None, None),
            P(None, "blk", None, None),
        ),
        out_specs=P("rhs", "blk"),
        check_vma=False,
    )
```

```python
import functools

import jax
import jax.numpy as jnp
from jax import lax
from jax.experimental import pallas as pl
from jax.experimental.pallas import tpu as pltpu
from jax.sharding import PartitionSpec as P

F32 = jnp.float32
BF16 = jnp.bfloat16
MESH = pl.DeviceIdType.MESH

WIDTH = 256
RANK = 32
BLOCKS = 8
RING = 8
ROWS = 8
ALL = ROWS * RING
LOWER = ALL + RANK
UPPER = LOWER + RANK
SHARE = WIDTH // RING
SLAB = 16
SLABS = 4
UNITS = 2 * BLOCKS
LANES = 128
PACK = LANES // RANK
VROWS = ALL // PACK
MAP = 8 + VROWS
HALVES = 2

ORDER = [(0, m) for m in range(BLOCKS)] + [(1, m) for m in reversed(range(BLOCKS))]


def pair_index(a, b):
    high, low = max(a, b), min(a, b)
    return high * (high - 1) // 2 + low


def parts(x):
    high = x.astype(BF16)
    return high, (x - high.astype(F32)).astype(BF16)


def times(a, b, trans):
    rows = a.shape[0]
    top = a.astype(BF16).astype(F32)
    stacked = jnp.concatenate([top, a - top], axis=0).astype(BF16)
    dims = (((1,), (1 if trans else 0,)), ((), ()))
    high, low = parts(b)
    p = lax.dot_general(stacked, high, dims, preferred_element_type=F32)
    q = lax.dot_general(stacked, low, dims, preferred_element_type=F32)
    p = p + q
    return p[:rows] + p[rows:]


def kernel(
    rhs_hbm, diag_hbm, left_hbm, right_hbm, rank_ref, pattern_ref, row_hbm, col_hbm,
    out_ref,
    rhs, inv, left, right, row, col, sol0, sol1, red, pack, xpack, result,
    load_sem, own_sem, unit_send, unit_recv, rhs_send, rhs_recv,
    slab_send, slab_recv, x_send, x_recv, out_send, out_recv, out_own,
):
    g = lax.axis_index("blk")
    y = lax.axis_index("rhs")
    slab, place = g // SLAB, g % SLAB
    home = (RING // 2) * (g % 2)
    barrier = pltpu.get_barrier_semaphore()

    def unit_copy(unit, origin):
        s, m = ORDER[unit]
        return pltpu.make_async_remote_copy(
            src_ref=diag_hbm.at[s, m],
            dst_ref=inv.at[s, m, pl.ds(SHARE * origin, SHARE), :],
            send_sem=unit_send.at[unit],
            recv_sem=unit_recv.at[unit, (origin - home + RING) % RING - 1],
            device_id=(g, home),
            device_id_type=MESH,
        )

    def rhs_copy(origin):
        return pltpu.make_async_remote_copy(
            src_ref=rhs_hbm,
            dst_ref=rhs.at[pl.ds(ROWS * origin, ROWS), :],
            send_sem=rhs_send,
            recv_sem=rhs_recv.at[(origin - home + RING) % RING - 1],
            device_id=(g, home),
            device_id_type=MESH,
        )

    width = out_ref.shape[1] // HALVES

    def out_copy(half, d):
        n = (home + d) % RING
        return pltpu.make_async_remote_copy(
            src_ref=result.at[pl.ds(ROWS * n, ROWS), pl.ds(half * width, width)],
            dst_ref=out_ref.at[:, pl.ds(half * width, width)],
            send_sem=out_send.at[half, d - 1],
            recv_sem=out_recv.at[half],
            device_id=(g, n),
            device_id_type=MESH,
        )

    @pl.when(y != home)
    def _():
        pl.semaphore_signal(barrier, inc=1, device_id=(g, home), device_id_type=MESH)
        pl.semaphore_wait(barrier, 1)
        rhs_copy(y).start()
        for unit in range(UNITS):
            unit_copy(unit, y).start()
        rhs_copy(y).wait_send()
        for unit in range(UNITS):
            unit_copy(unit, y).wait_send()
        for half in range(HALVES):
            out_copy(half, 1).wait_recv()

    @pl.when(y == home)
    def _():
        solve_group(
            g, y, slab, place, home, barrier, unit_copy, rhs_copy, out_copy,
            rhs_hbm, diag_hbm, left_hbm, right_hbm, rank_ref, pattern_ref, row_hbm, col_hbm,
            out_ref,
            rhs, inv, left, right, row, col, sol0, sol1, red, pack, xpack, result,
            load_sem, own_sem, slab_send, slab_recv, x_send, x_recv, out_own,
        )


def solve_group(
    g, y, slab, place, home, barrier, unit_copy, rhs_copy, out_copy,
    rhs_hbm, diag_hbm, left_hbm, right_hbm, rank_ref, pattern_ref, row_hbm, col_hbm,
    out_ref,
    rhs, inv, left, right, row, col, sol0, sol1, red, pack, xpack, result,
    load_sem, own_sem, slab_send, slab_recv, x_send, x_recv, out_own,
):
    for d in range(1, RING):
        pl.semaphore_signal(
            barrier, inc=1, device_id=(g, (home + d) % RING), device_id_type=MESH
        )

    def slab_peer(d):
        there = (place + d) % SLAB
        return (slab * SLAB + there, (RING // 2) * (there % 2))

    def x_peer(d):
        return (((slab + d) % SLABS) * SLAB + place, home)

    for d in range(1, SLAB):
        pl.semaphore_signal(barrier, inc=1, device_id=slab_peer(d), device_id_type=MESH)
    for d in range(1, SLABS):
        pl.semaphore_signal(barrier, inc=1, device_id=x_peer(d), device_id_type=MESH)

    loads = [[], []]
    loads[0].append(
        pltpu.make_async_copy(rhs_hbm, rhs.at[pl.ds(ROWS * y, ROWS), :], load_sem.at[8])
    )
    for s in range(2):
        for i, (src, dst) in enumerate(
            ((row_hbm, row), (col_hbm, col), (left_hbm, left), (right_hbm, right))
        ):
            loads[s].append(pltpu.make_async_copy(src.at[s], dst.at[s], load_sem.at[4 * s + i]))
        loads[s].append(
            pltpu.make_async_copy(
                diag_hbm.at[s], inv.at[s, :, pl.ds(SHARE * y, SHARE), :], own_sem.at[s]
            )
        )
    for s in range(2):
        for c in loads[s]:
            c.start()

    lane = lax.broadcasted_iota(jnp.int32, (8, WIDTH), 1)
    slot_of, within = lane // RANK, lane % RANK
    lane128 = lax.broadcasted_iota(jnp.int32, (8, LANES), 1)
    sub128 = lax.broadcasted_iota(jnp.int32, (8, LANES), 0)
    totals = [jnp.zeros((LOWER, LANES), F32), jnp.zeros((UPPER, LANES), F32)]

    def solve(unit):
        s, m = ORDER[unit]
        rows = LOWER if s == 0 else UPPER
        earlier = list(range(m)) if s == 0 else list(range(m + 1, BLOCKS))
        later = list(range(m + 1, BLOCKS)) if s == 0 else list(range(m))
        if s == 0:
            side = jnp.concatenate([rhs[:, m * WIDTH : (m + 1) * WIDTH], -row[0, m]], axis=0)
        else:
            side = jnp.concatenate([sol0[m], -row[1, m]], axis=0)
        if earlier:
            ranks = jnp.zeros((8, WIDTH), jnp.int32)
            reduced = jnp.zeros((rows, WIDTH), F32)
            for k in earlier:
                p = pair_index(m, k)
                rank = jnp.where(pattern_ref[s, p] == 1, rank_ref[s, p], 0)
                ranks = jnp.where(slot_of == (m ^ k), rank, ranks)
                hit = jnp.tile(slot_of == (m ^ k), (rows // 8, 1))
                reduced = jnp.where(hit, red[k, :rows, :], reduced)
            keep = jnp.where(within < ranks, 1.0, 0.0).astype(F32)
            reduced = reduced * jnp.tile(keep, (rows // 8, 1))
            tiles = [
                left[s, pair_index(m, m ^ j)] if (m ^ j) in earlier else jnp.zeros((RANK, WIDTH), F32)
                for j in range(BLOCKS)
            ]
            side = side - times(reduced, jnp.concatenate(tiles, axis=0), False)
        for d in range(1, RING):
            unit_copy(unit, (home + d) % RING).wait_recv()
        solved = times(side, inv[s, m], True)
        if s == 0:
            sol0[m] = solved
        else:
            sol1[m] = solved
        tiles = [col[s, m]] + [
            right[s, pair_index(m, m ^ j)] if (m ^ j) in later else jnp.zeros((RANK, WIDTH), F32)
            for j in range(1, BLOCKS)
        ]
        if later:
            after = times(solved, jnp.concatenate(tiles, axis=0), True)
            red[m, :rows, :] = after
            totals[s] = totals[s] + after[:, :LANES]
        else:
            after = times(solved, jnp.concatenate(tiles[:PACK], axis=0), True)
            totals[s] = totals[s] + after

    low_lanes = lane128 < RANK
    low_tall = jnp.tile(low_lanes, (ALL // 8, 1))
    unit_pack = jnp.concatenate(
        [
            jnp.where(lane128 % RANK == sub128 + 8 * (lane128 // RANK), 1.0, 0.0).astype(F32),
            jnp.zeros((VROWS, LANES), F32),
        ],
        axis=0,
    )
    only_v = jnp.concatenate([jnp.zeros((8, LANES), F32), jnp.ones((VROWS, LANES), F32)], axis=0)

    def turned(x, groups):
        groups = groups % PACK
        return pltpu.roll(x, RANK * groups, 1) if groups else x

    def beside(x, group_rows):
        x = jnp.where(low_tall[: x.shape[0]], x, 0.0)
        total = x[:group_rows]
        for i in range(1, PACK):
            total = total + turned(x[group_rows * i : group_rows * (i + 1)], i)
        return total

    def packed(gain_rows, v):
        return jnp.concatenate([unit_pack[:8] + beside(gain_rows, 8), beside(v, VROWS)], axis=0)

    def below(v):
        stacked = jnp.concatenate([turned(v, PACK - i) for i in range(PACK)], axis=0)
        return jnp.where(low_tall, stacked, 0.0)

    def spread(m):
        a = m[:8]
        rolled = [turned(a, i) for i in range(PACK)]
        strips = []
        for b in range(PACK):
            for i in range(PACK):
                strips.append(jnp.where(lane128 // RANK == b, rolled[(b - i) % PACK], 0.0))
        return jnp.concatenate(strips, axis=0)

    def after(first, then):
        return times(first, spread(then), False) + then * only_v

    def slab_copy(s, d):
        return pltpu.make_async_remote_copy(
            src_ref=pack.at[s, place],
            dst_ref=pack.at[s, place],
            send_sem=slab_send.at[s, d - 1],
            recv_sem=slab_recv.at[s, d - 1],
            device_id=slab_peer(d),
            device_id_type=MESH,
        )

    def slab_arrived(s, d):
        here = pack.at[s, (place + SLAB - d) % SLAB]
        pltpu.make_async_remote_copy(
            src_ref=here,
            dst_ref=here,
            send_sem=slab_send.at[s, d - 1],
            recv_sem=slab_recv.at[s, d - 1],
            device_id=slab_peer(d),
            device_id_type=MESH,
        ).wait_recv()

    def x_copy(s, d):
        return pltpu.make_async_remote_copy(
            src_ref=xpack.at[s, slab],
            dst_ref=xpack.at[s, slab],
            send_sem=x_send.at[s, d - 1],
            recv_sem=x_recv.at[s, d - 1],
            device_id=x_peer(d),
            device_id_type=MESH,
        )

    def x_arrived(s, d):
        here = xpack.at[s, (slab + SLABS - d) % SLABS]
        pltpu.make_async_remote_copy(
            src_ref=here,
            dst_ref=here,
            send_sem=x_send.at[s, d - 1],
            recv_sem=x_recv.at[s, d - 1],
            device_id=x_peer(d),
            device_id_type=MESH,
        ).wait_recv()

    def exchange_start(s, packet):
        pack[s, place] = packet
        for d in range(1, SLAB):
            slab_copy(s, d).start()

    def exchange_middle(s):
        for d in range(1, SLAB):
            slab_arrived(s, d)
        mine = place if s == 0 else SLAB - 1 - place
        nodes = [pack[s, i if s == 0 else SLAB - 1 - i] for i in range(SLAB)]
        ahead = None
        while len(nodes) > 1:
            left_one = unit_pack
            size = SLAB // len(nodes)
            for i in range(0, len(nodes), 2):
                at = mine // size == i + 1
                left_one = jnp.where(at, nodes[i], left_one)
            nodes = [after(nodes[i], nodes[i + 1]) for i in range(0, len(nodes), 2)]
            ahead = left_one if ahead is None else after(left_one, ahead)
        xpack[s, slab] = nodes[0]
        for d in range(1, SLABS):
            x_copy(s, d).start()
        return ahead

    def exchange_end(s, ahead):
        wide = spread(ahead)
        for d in range(1, SLABS):
            x_arrived(s, d)
        order = list(range(SLABS)) if s == 0 else list(reversed(range(SLABS)))
        maps = [
            jnp.where((slab > i) if s == 0 else (slab < i), xpack[s, i], unit_pack) for i in order
        ]
        entering = maps[0][8:]
        for one in maps[1 : SLABS - 1]:
            entering = times(entering, spread(one), False) + one[8:]
        return times(entering, wide, False) + ahead[8:]

    ahead, carried = None, None
    for unit in range(UNITS):
        if unit == 0:
            for c in loads[0]:
                c.wait()
            for d in range(1, RING):
                rhs_copy((home + d) % RING).wait_recv()
        if unit == BLOCKS:
            for c in loads[1]:
                c.wait()
        solve(unit)
        if unit == BLOCKS - 1:
            pl.semaphore_wait(barrier, RING - 1 + SLAB - 1 + SLABS - 1)
            exchange_start(0, packed(totals[0][ALL:], totals[0][:ALL]))
        if unit == BLOCKS + 2:
            ahead = exchange_middle(0)
        if unit == BLOCKS + 5:
            carried = below(exchange_end(0, ahead))

    upper_v = totals[1][:ALL] + times(carried[:, :RANK], totals[1][ALL:LOWER], False)
    exchange_start(1, packed(totals[1][LOWER:], upper_v))
    entering = below(exchange_end(1, exchange_middle(1)))

    both = (carried + turned(entering, 1))[:, : 2 * RANK]
    own = []
    for half in range(HALVES):
        for m in range(half * BLOCKS // HALVES, (half + 1) * BLOCKS // HALVES):
            result[:, m * WIDTH : (m + 1) * WIDTH] = sol1[m, :ALL, :] + times(
                both, sol1[m, ALL:, :], False
            )
        for d in range(1, RING):
            out_copy(half, d).start()
        part = pl.ds(half * (BLOCKS // HALVES) * WIDTH, (BLOCKS // HALVES) * WIDTH)
        own.append(
            pltpu.make_async_copy(
                result.at[pl.ds(ROWS * y, ROWS), part], out_ref.at[:, part], out_own.at[half]
            )
        )
        own[half].start()

    for s in range(2):
        for d in range(1, SLAB):
            slab_copy(s, d).wait_send()
        for d in range(1, SLABS):
            x_copy(s, d).wait_send()
    for half in range(HALVES):
        own[half].wait()
        for d in range(1, RING):
            out_copy(half, d).wait_send()


def shards(rhs, diag, left, right, rank, pattern, row, col):
    hbm = pl.BlockSpec(memory_space=pl.ANY)
    smem = pl.BlockSpec(memory_space=pltpu.SMEM)
    return pl.pallas_call(
        kernel,
        out_shape=jax.ShapeDtypeStruct(rhs.shape, F32),
        in_specs=[hbm, hbm, hbm, hbm, smem, smem, hbm, hbm],
        out_specs=hbm,
        scratch_shapes=[
            pltpu.VMEM((ALL, rhs.shape[1]), F32),
            pltpu.VMEM((2, BLOCKS, WIDTH, WIDTH), F32),
            pltpu.VMEM(left.shape, F32),
            pltpu.VMEM(right.shape, F32),
            pltpu.VMEM(row.shape, F32),
            pltpu.VMEM(col.shape, F32),
            pltpu.VMEM((BLOCKS, LOWER, WIDTH), F32),
            pltpu.VMEM((BLOCKS, UPPER, WIDTH), F32),
            pltpu.VMEM((BLOCKS, UPPER, WIDTH), F32),
            pltpu.VMEM((2, SLAB, MAP, LANES), F32),
            pltpu.VMEM((2, SLABS, MAP, LANES), F32),
            pltpu.VMEM((ALL, rhs.shape[1]), F32),
            pltpu.SemaphoreType.DMA((9,)),
            pltpu.SemaphoreType.DMA((2,)),
            pltpu.SemaphoreType.DMA((UNITS,)),
            pltpu.SemaphoreType.DMA((UNITS, RING - 1)),
            pltpu.SemaphoreType.DMA,
            pltpu.SemaphoreType.DMA((RING - 1,)),
            pltpu.SemaphoreType.DMA((2, SLAB - 1)),
            pltpu.SemaphoreType.DMA((2, SLAB - 1)),
            pltpu.SemaphoreType.DMA((2, SLABS - 1)),
            pltpu.SemaphoreType.DMA((2, SLABS - 1)),
            pltpu.SemaphoreType.DMA((HALVES, RING - 1)),
            pltpu.SemaphoreType.DMA((HALVES,)),
            pltpu.SemaphoreType.DMA((HALVES,)),
        ],
        compiler_params=pltpu.CompilerParams(
            collective_id=0, has_side_effects=True, vmem_limit_bytes=60 * 1024 * 1024
        ),
        cost_estimate=pl.CostEstimate(
            flops=400_000_000, bytes_accessed=6_000_000, transcendentals=0
        ),
    )(rhs, diag, left, right, rank, pattern, row, col)


def solution(mesh):
    return jax.shard_map(
        shards,
        mesh=mesh,
        in_specs=(
            P("rhs", "blk"),
            P(None, "blk", "rhs", None),
            P(None, "blk", None, None),
            P(None, "blk", None, None),
            P(None, "blk"),
            P(None, "blk"),
            P(None, "blk", None, None),
            P(None, "blk", None, None),
        ),
        out_specs=P("rhs", "blk"),
        check_vma=False,
    )
```

```python
import functools

import jax
import jax.numpy as jnp
from jax import lax
from jax.experimental import pallas as pl
from jax.experimental.pallas import tpu as pltpu
from jax.sharding import PartitionSpec as P

F32 = jnp.float32
BF16 = jnp.bfloat16
MESH = pl.DeviceIdType.MESH

WIDTH = 256
RANK = 32
BLOCKS = 8
RING = 8
ROWS = 8
ALL = ROWS * RING
LOWER = ALL + RANK
UPPER = LOWER + RANK
SHARE = WIDTH // RING
OCTET = 8
UNITS = 2 * BLOCKS
LANES = 128
PACK = LANES // RANK
VROWS = ALL // PACK
MAP = 8 + VROWS
PARTS = 4
WINDOW = 6
STRIDE = 2

ORDER = [(0, m) for m in range(BLOCKS)] + [(1, m) for m in reversed(range(BLOCKS))]


def pair_index(a, b):
    high, low = max(a, b), min(a, b)
    return high * (high - 1) // 2 + low


def parts(x):
    high = x.astype(BF16)
    return high, (x - high.astype(F32)).astype(BF16)


def times(a, b, trans):
    rows = a.shape[0]
    top = a.astype(BF16).astype(F32)
    stacked = jnp.concatenate([top, a - top], axis=0).astype(BF16)
    dims = (((1,), (1 if trans else 0,)), ((), ()))
    high, low = parts(b)
    p = lax.dot_general(stacked, high, dims, preferred_element_type=F32)
    q = lax.dot_general(a.astype(BF16), low, dims, preferred_element_type=F32)
    return p[:rows] + (p[rows:] + q)


def kernel(
    rhs_hbm, diag_hbm, left_hbm, right_hbm, rank_ref, pattern_ref, row_hbm, col_hbm,
    out_ref,
    rhs, inv, left, right, row, col, sol0, sol1, red, pack, result,
    load_sem, own_sem, unit_send, unit_recv, rhs_send, rhs_recv,
    map_send, map_recv, out_send, out_recv, go_sem,
):
    g = lax.axis_index("blk")
    y = lax.axis_index("rhs")
    places = (g % OCTET, g // OCTET)
    home = (RING // 2) * (g % 2)
    barrier = pltpu.get_barrier_semaphore()

    def unit_copy(unit, origin):
        s, m = ORDER[unit]
        return pltpu.make_async_remote_copy(
            src_ref=diag_hbm.at[s, m],
            dst_ref=inv.at[s, m, pl.ds(SHARE * origin, SHARE), :],
            send_sem=unit_send.at[unit],
            recv_sem=unit_recv.at[unit, (origin - home + RING) % RING - 1],
            device_id=(g, home),
            device_id_type=MESH,
        )

    def rhs_copy(origin):
        return pltpu.make_async_remote_copy(
            src_ref=rhs_hbm,
            dst_ref=rhs.at[pl.ds(ROWS * origin, ROWS), :],
            send_sem=rhs_send,
            recv_sem=rhs_recv.at[(origin - home + RING) % RING - 1],
            device_id=(g, home),
            device_id_type=MESH,
        )

    width = out_ref.shape[1] // PARTS

    def out_copy(part, d):
        n = (home + d) % RING
        return pltpu.make_async_remote_copy(
            src_ref=result.at[pl.ds(ROWS * n, ROWS), pl.ds(part * width, width)],
            dst_ref=out_ref.at[:, pl.ds(part * width, width)],
            send_sem=out_send.at[part, d - 1],
            recv_sem=out_recv.at[part],
            device_id=(g, n),
            device_id_type=MESH,
        )

    @pl.when(y != home)
    def _():
        pl.semaphore_signal(barrier, inc=1, device_id=(g, home), device_id_type=MESH)
        pl.semaphore_wait(barrier, 1)
        rhs_copy(y).start()
        for unit in range(UNITS):
            if unit >= WINDOW and unit % STRIDE == 0:
                pl.semaphore_wait(go_sem, 1)
            unit_copy(unit, y).start()
        rhs_copy(y).wait_send()
        for unit in range(UNITS):
            unit_copy(unit, y).wait_send()
        for part in range(PARTS):
            out_copy(part, 1).wait_recv()

    @pl.when(y == home)
    def _():
        solve_group(
            g, y, places, home, barrier, unit_copy, rhs_copy, out_copy,
            rhs_hbm, diag_hbm, left_hbm, right_hbm, rank_ref, pattern_ref, row_hbm, col_hbm,
            out_ref,
            rhs, inv, left, right, row, col, sol0, sol1, red, pack, result,
            load_sem, own_sem, map_send, map_recv, go_sem,
        )


def solve_group(
    g, y, places, home, barrier, unit_copy, rhs_copy, out_copy,
    rhs_hbm, diag_hbm, left_hbm, right_hbm, rank_ref, pattern_ref, row_hbm, col_hbm,
    out_ref,
    rhs, inv, left, right, row, col, sol0, sol1, red, pack, result,
    load_sem, own_sem, map_send, map_recv, go_sem,
):
    for d in range(1, RING):
        pl.semaphore_signal(
            barrier, inc=1, device_id=(g, (home + d) % RING), device_id_type=MESH
        )

    def peer(stage, d):
        there = (places[stage] + d) % OCTET
        if stage == 0:
            return (places[1] * OCTET + there, (RING // 2) * (there % 2))
        return (there * OCTET + places[0], home)

    for stage in range(2):
        for d in range(1, OCTET):
            pl.semaphore_signal(barrier, inc=1, device_id=peer(stage, d), device_id_type=MESH)

    loads = [[], []]
    loads[0].append(
        pltpu.make_async_copy(rhs_hbm, rhs.at[pl.ds(ROWS * y, ROWS), :], load_sem.at[8])
    )
    for s in range(2):
        for i, (src, dst) in enumerate(
            ((row_hbm, row), (col_hbm, col), (left_hbm, left), (right_hbm, right))
        ):
            loads[s].append(pltpu.make_async_copy(src.at[s], dst.at[s], load_sem.at[4 * s + i]))
        loads[s].append(
            pltpu.make_async_copy(
                diag_hbm.at[s], inv.at[s, :, pl.ds(SHARE * y, SHARE), :], own_sem.at[s]
            )
        )
    for s in range(2):
        for c in loads[s]:
            c.start()

    lane128 = lax.broadcasted_iota(jnp.int32, (8, LANES), 1)
    slot_of, within = lane128 // RANK, lane128 % RANK
    sub128 = lax.broadcasted_iota(jnp.int32, (8, LANES), 0)
    totals = [jnp.zeros((LOWER, LANES), F32), jnp.zeros((UPPER, LANES), F32)]

    def solve(unit):
        s, m = ORDER[unit]
        rows = LOWER if s == 0 else UPPER
        earlier = list(range(m)) if s == 0 else list(range(m + 1, BLOCKS))
        later = list(range(m + 1, BLOCKS)) if s == 0 else list(range(m))
        if s == 0:
            side = jnp.concatenate([rhs[:, m * WIDTH : (m + 1) * WIDTH], -row[0, m]], axis=0)
        else:
            side = jnp.concatenate([sol0[m], -row[1, m]], axis=0)
        if earlier:
            reduced, tiles = [], []
            for h in sorted({(m ^ k) // PACK for k in earlier}):
                ranks = jnp.zeros((8, LANES), jnp.int32)
                piece = jnp.zeros((rows, LANES), F32)
                for j in range(h * PACK, (h + 1) * PACK):
                    k = m ^ j
                    if k not in earlier:
                        tiles.append(jnp.zeros((RANK, WIDTH), F32))
                        continue
                    p = pair_index(m, k)
                    tiles.append(left[s, p])
                    rank = jnp.where(pattern_ref[s, p] == 1, rank_ref[s, p], 0)
                    hit = slot_of == j - h * PACK
                    ranks = jnp.where(hit, rank, ranks)
                    from_k = red[k, :rows, h * LANES : (h + 1) * LANES]
                    piece = jnp.where(jnp.tile(hit, (rows // 8, 1)), from_k, piece)
                keep = jnp.where(within < ranks, 1.0, 0.0).astype(F32)
                reduced.append(piece * jnp.tile(keep, (rows // 8, 1)))
            reduced = jnp.concatenate(reduced, axis=1)
            side = side - times(reduced, jnp.concatenate(tiles, axis=0), False)
        for d in range(1, RING):
            unit_copy(unit, (home + d) % RING).wait_recv()
        if unit == STRIDE - 1:
            pl.semaphore_wait(barrier, RING - 1 + 2 * (OCTET - 1))
        if unit % STRIDE == STRIDE - 1 and unit + WINDOW - STRIDE < UNITS - 1:
            for d in range(1, RING):
                pl.semaphore_signal(
                    go_sem, inc=1, device_id=(g, (home + d) % RING), device_id_type=MESH
                )
        solved = times(side, inv[s, m], True)
        if s == 0:
            sol0[m] = solved
        else:
            sol1[m] = solved
        tiles = [col[s, m]] + [
            right[s, pair_index(m, m ^ j)] if (m ^ j) in later else jnp.zeros((RANK, WIDTH), F32)
            for j in range(1, BLOCKS)
        ]
        count = BLOCKS if any((m ^ k) >= PACK for k in later) else PACK
        onward = times(solved, jnp.concatenate(tiles[:count], axis=0), True)
        if later:
            red[m, :rows, : count * RANK] = onward
        totals[s] = totals[s] + onward[:, :LANES]

    low_lanes = lane128 < RANK
    low_tall = jnp.tile(low_lanes, (ALL // 8, 1))
    unit_pack = jnp.concatenate(
        [
            jnp.where(lane128 % RANK == sub128 + 8 * (lane128 // RANK), 1.0, 0.0).astype(F32),
            jnp.zeros((VROWS, LANES), F32),
        ],
        axis=0,
    )
    only_v = jnp.concatenate([jnp.zeros((8, LANES), F32), jnp.ones((VROWS, LANES), F32)], axis=0)

    def turned(x, groups):
        groups = groups % PACK
        return pltpu.roll(x, RANK * groups, 1) if groups else x

    def beside(x, group_rows):
        x = jnp.where(low_tall[: x.shape[0]], x, 0.0)
        total = x[:group_rows]
        for i in range(1, PACK):
            total = total + turned(x[group_rows * i : group_rows * (i + 1)], i)
        return total

    def packed(gain_rows, v):
        return jnp.concatenate([unit_pack[:8] + beside(gain_rows, 8), beside(v, VROWS)], axis=0)

    def below(v):
        stacked = jnp.concatenate([turned(v, PACK - i) for i in range(PACK)], axis=0)
        return jnp.where(low_tall, stacked, 0.0)

    def spread(m):
        a = m[:8]
        rolled = [turned(a, i) for i in range(PACK)]
        strips = []
        for b in range(PACK):
            for i in range(PACK):
                strips.append(jnp.where(lane128 // RANK == b, rolled[(b - i) % PACK], 0.0))
        return jnp.concatenate(strips, axis=0)

    def after(first, then):
        return times(first, spread(then), False) + then * only_v

    def map_copy(s, stage, d):
        return pltpu.make_async_remote_copy(
            src_ref=pack.at[s, stage, places[stage]],
            dst_ref=pack.at[s, stage, places[stage]],
            send_sem=map_send.at[s, stage, d - 1],
            recv_sem=map_recv.at[s, stage, d - 1],
            device_id=peer(stage, d),
            device_id_type=MESH,
        )

    def map_arrived(s, stage, d):
        here = pack.at[s, stage, (places[stage] + OCTET - d) % OCTET]
        pltpu.make_async_remote_copy(
            src_ref=here,
            dst_ref=here,
            send_sem=map_send.at[s, stage, d - 1],
            recv_sem=map_recv.at[s, stage, d - 1],
            device_id=peer(stage, d),
            device_id_type=MESH,
        ).wait_recv()

    def send_map(s, stage, one):
        pack[s, stage, places[stage]] = one
        for d in range(1, OCTET):
            map_copy(s, stage, d).start()

    def join_maps(s, stage):
        for d in range(1, OCTET):
            map_arrived(s, stage, d)
        mine = places[stage] if s == 0 else OCTET - 1 - places[stage]
        nodes = [pack[s, stage, i if s == 0 else OCTET - 1 - i] for i in range(OCTET)]
        ahead = None
        while len(nodes) > 1:
            left_one = unit_pack
            size = OCTET // len(nodes)
            for i in range(0, len(nodes), 2):
                left_one = jnp.where(mine // size == i + 1, nodes[i], left_one)
            if len(nodes) > 2 or stage == 0:
                nodes = [after(nodes[i], nodes[i + 1]) for i in range(0, len(nodes), 2)]
            else:
                nodes = nodes[:1]
            ahead = left_one if ahead is None else after(left_one, ahead)
        return nodes[0], ahead

    near, carried = None, None
    for unit in range(UNITS):
        if unit == 0:
            for c in loads[0]:
                c.wait()
            for d in range(1, RING):
                rhs_copy((home + d) % RING).wait_recv()
        if unit == BLOCKS:
            for c in loads[1]:
                c.wait()
        solve(unit)
        if unit == BLOCKS - 1:
            send_map(0, 0, packed(totals[0][ALL:], totals[0][:ALL]))
        if unit == BLOCKS + 2:
            whole, near = join_maps(0, 0)
            send_map(0, 1, whole)
        if unit == BLOCKS + 5:
            carried = below(after(join_maps(0, 1)[1], near)[8:])

    early = turned(carried, ALL // RANK)
    upper_v = totals[1][:ALL] + times(early, totals[1], False)
    send_map(1, 0, packed(totals[1][LOWER:], upper_v))
    for m in range(BLOCKS):
        sol1[m, :ALL, :] = sol1[m, :ALL, :] + times(early, sol1[m], False)
    whole, near = join_maps(1, 0)
    send_map(1, 1, whole)
    entering = below(after(join_maps(1, 1)[1], near)[8:])

    late = turned(entering, LOWER // RANK)
    for part in range(PARTS):
        for m in range(part * BLOCKS // PARTS, (part + 1) * BLOCKS // PARTS):
            result[:, m * WIDTH : (m + 1) * WIDTH] = sol1[m, :ALL, :] + times(
                late, sol1[m], False
            )
        for d in range(1, RING):
            out_copy(part, d).start()
    out_ref[...] = result[pl.ds(pl.multiple_of(ROWS * y, ROWS), ROWS), :]

    for s in range(2):
        for stage in range(2):
            for d in range(1, OCTET):
                map_copy(s, stage, d).wait_send()
    for part in range(PARTS):
        for d in range(1, RING):
            out_copy(part, d).wait_send()


def shards(rhs, diag, left, right, rank, pattern, row, col):
    hbm = pl.BlockSpec(memory_space=pl.ANY)
    smem = pl.BlockSpec(memory_space=pltpu.SMEM)
    return pl.pallas_call(
        kernel,
        out_shape=jax.ShapeDtypeStruct(rhs.shape, F32),
        in_specs=[hbm, hbm, hbm, hbm, smem, smem, hbm, hbm],
        out_specs=pl.BlockSpec(memory_space=pltpu.VMEM),
        scratch_shapes=[
            pltpu.VMEM((ALL, rhs.shape[1]), F32),
            pltpu.VMEM((2, BLOCKS, WIDTH, WIDTH), F32),
            pltpu.VMEM(left.shape, F32),
            pltpu.VMEM(right.shape, F32),
            pltpu.VMEM(row.shape, F32),
            pltpu.VMEM(col.shape, F32),
            pltpu.VMEM((BLOCKS, LOWER, WIDTH), F32),
            pltpu.VMEM((BLOCKS, UPPER, WIDTH), F32),
            pltpu.VMEM((BLOCKS, UPPER, WIDTH), F32),
            pltpu.VMEM((2, 2, OCTET, MAP, LANES), F32),
            pltpu.VMEM((ALL, rhs.shape[1]), F32),
            pltpu.SemaphoreType.DMA((9,)),
            pltpu.SemaphoreType.DMA((2,)),
            pltpu.SemaphoreType.DMA((UNITS,)),
            pltpu.SemaphoreType.DMA((UNITS, RING - 1)),
            pltpu.SemaphoreType.DMA,
            pltpu.SemaphoreType.DMA((RING - 1,)),
            pltpu.SemaphoreType.DMA((2, 2, OCTET - 1)),
            pltpu.SemaphoreType.DMA((2, 2, OCTET - 1)),
            pltpu.SemaphoreType.DMA((PARTS, RING - 1)),
            pltpu.SemaphoreType.DMA((PARTS,)),
            pltpu.SemaphoreType.REGULAR,
        ],
        compiler_params=pltpu.CompilerParams(
            collective_id=0, has_side_effects=True, vmem_limit_bytes=60 * 1024 * 1024
        ),
        cost_estimate=pl.CostEstimate(
            flops=400_000_000, bytes_accessed=6_000_000, transcendentals=0
        ),
    )(rhs, diag, left, right, rank, pattern, row, col)


def solution(mesh):
    return jax.shard_map(
        shards,
        mesh=mesh,
        in_specs=(
            P("rhs", "blk"),
            P(None, "blk", "rhs", None),
            P(None, "blk", None, None),
            P(None, "blk", None, None),
            P(None, "blk"),
            P(None, "blk"),
            P(None, "blk", None, None),
            P(None, "blk", None, None),
        ),
        out_specs=P("rhs", "blk"),
        check_vma=False,
    )
```

```python
import functools

import jax
import jax.numpy as jnp
from jax import lax
from jax.experimental import pallas as pl
from jax.experimental.pallas import tpu as pltpu
from jax.sharding import PartitionSpec as P

F32 = jnp.float32
BF16 = jnp.bfloat16
MESH = pl.DeviceIdType.MESH

WIDTH = 256
RANK = 32
BLOCKS = 8
RING = 8
ROWS = 8
ALL = ROWS * RING
LOWER = ALL + RANK
UPPER = LOWER + RANK
SHARE = WIDTH // RING
OCTET = 8
UNITS = 2 * BLOCKS
LANES = 128
PACK = LANES // RANK
VROWS = ALL // PACK
MAP = 8 + VROWS
FAR_FIRST = (4, 5, 3, 6, 2, 7, 1)
PARTS = 4
WINDOW = 8
RELAYED = (1, 3, 5, 7, 9, 11, 13)
OPPOSITE, BESIDE = RING // 2, RING // 2 - 1
DELAY = 2
STRIDE = 2

ORDER = [(0, m) for m in range(BLOCKS)] + [(1, m) for m in reversed(range(BLOCKS))]


def pair_index(a, b):
    high, low = max(a, b), min(a, b)
    return high * (high - 1) // 2 + low


def parts(x):
    high = x.astype(BF16)
    return high, (x - high.astype(F32)).astype(BF16)


def times(a, b, trans):
    rows = a.shape[0]
    top = a.astype(BF16).astype(F32)
    stacked = jnp.concatenate([top, a - top], axis=0).astype(BF16)
    dims = (((1,), (1 if trans else 0,)), ((), ()))
    high, low = parts(b)
    p = lax.dot_general(stacked, high, dims, preferred_element_type=F32)
    q = lax.dot_general(a.astype(BF16), low, dims, preferred_element_type=F32)
    return p[:rows] + (p[rows:] + q)


def kernel(
    rhs_hbm, diag_hbm, left_hbm, right_hbm, rank_ref, pattern_ref, row_hbm, col_hbm,
    out_ref,
    rhs, inv, left, right, row, col, sol0, sol1, red, pack, result,
    load_sem, own_sem, unit_send, unit_recv, rhs_send, rhs_recv,
    map_send, map_recv, out_send, out_recv, go_sem, relay_send, relay_recv,
):
    g = lax.axis_index("blk")
    y = lax.axis_index("rhs")
    places = (g % OCTET, g // OCTET)
    home = (RING // 2) * (g % 2)
    barrier = pltpu.get_barrier_semaphore()

    def unit_copy(unit, origin):
        s, m = ORDER[unit]
        return pltpu.make_async_remote_copy(
            src_ref=diag_hbm.at[s, m],
            dst_ref=inv.at[s, m, pl.ds(SHARE * origin, SHARE), :],
            send_sem=unit_send.at[unit],
            recv_sem=unit_recv.at[unit, (origin - home + RING) % RING - 1],
            device_id=(g, home),
            device_id_type=MESH,
        )

    far = (home + OPPOSITE) % RING

    def relay_copy(unit, hop):
        s, m = ORDER[unit]
        here = inv.at[s, m, pl.ds(SHARE * far, SHARE), :]
        return pltpu.make_async_remote_copy(
            src_ref=diag_hbm.at[s, m] if hop == 0 else here,
            dst_ref=here,
            send_sem=unit_send.at[unit] if hop == 0 else relay_send.at[unit],
            recv_sem=relay_recv.at[unit] if hop == 0 else unit_recv.at[unit, OPPOSITE - 1],
            device_id=(g, (home + BESIDE) % RING if hop == 0 else home),
            device_id_type=MESH,
        )

    def rhs_copy(origin):
        return pltpu.make_async_remote_copy(
            src_ref=rhs_hbm,
            dst_ref=rhs.at[pl.ds(ROWS * origin, ROWS), :],
            send_sem=rhs_send,
            recv_sem=rhs_recv.at[(origin - home + RING) % RING - 1],
            device_id=(g, home),
            device_id_type=MESH,
        )

    width = out_ref.shape[1] // PARTS

    def out_copy(part, d):
        n = (home + d) % RING
        return pltpu.make_async_remote_copy(
            src_ref=result.at[pl.ds(ROWS * n, ROWS), pl.ds(part * width, width)],
            dst_ref=out_ref.at[:, pl.ds(part * width, width)],
            send_sem=out_send.at[part, d - 1],
            recv_sem=out_recv.at[part],
            device_id=(g, n),
            device_id_type=MESH,
        )

    @pl.when(y != home)
    def _():
        step = (y - home + RING) % RING
        pl.semaphore_signal(barrier, inc=1, device_id=(g, home), device_id_type=MESH)

        @pl.when(step == BESIDE)
        def _():
            pl.semaphore_signal(barrier, inc=1, device_id=(g, far), device_id_type=MESH)

        pl.semaphore_wait(barrier, jnp.where(step == OPPOSITE, 2, 1))
        rhs_copy(y).start()
        for unit in range(UNITS):
            if unit >= WINDOW and unit % STRIDE == 0:
                pl.semaphore_wait(go_sem, 1)
            if unit in RELAYED:

                @pl.when(step == OPPOSITE)
                def _():
                    relay_copy(unit, 0).start()

                @pl.when(step != OPPOSITE)
                def _():
                    unit_copy(unit, y).start()

            else:
                unit_copy(unit, y).start()
            if unit - DELAY in RELAYED:

                @pl.when(step == BESIDE)
                def _():
                    relay_copy(unit - DELAY, 0).wait_recv()
                    relay_copy(unit - DELAY, 1).start()

        rhs_copy(y).wait_send()
        for unit in range(UNITS):
            unit_copy(unit, y).wait_send()

        @pl.when(step == BESIDE)
        def _():
            for unit in RELAYED:
                relay_copy(unit, 1).wait_send()

        for part in range(PARTS):
            out_copy(part, 1).wait_recv()

    @pl.when(y == home)
    def _():
        solve_group(
            g, y, places, home, barrier, unit_copy, rhs_copy, out_copy,
            rhs_hbm, diag_hbm, left_hbm, right_hbm, rank_ref, pattern_ref, row_hbm, col_hbm,
            out_ref,
            rhs, inv, left, right, row, col, sol0, sol1, red, pack, result,
            load_sem, own_sem, map_send, map_recv, go_sem,
        )


def solve_group(
    g, y, places, home, barrier, unit_copy, rhs_copy, out_copy,
    rhs_hbm, diag_hbm, left_hbm, right_hbm, rank_ref, pattern_ref, row_hbm, col_hbm,
    out_ref,
    rhs, inv, left, right, row, col, sol0, sol1, red, pack, result,
    load_sem, own_sem, map_send, map_recv, go_sem,
):
    for d in range(1, RING):
        pl.semaphore_signal(
            barrier, inc=1, device_id=(g, (home + d) % RING), device_id_type=MESH
        )

    def peer(stage, d):
        there = (places[stage] + d) % OCTET
        if stage == 0:
            return (places[1] * OCTET + there, (RING // 2) * (there % 2))
        return (there * OCTET + places[0], home)

    for stage in range(2):
        for d in range(1, OCTET):
            pl.semaphore_signal(barrier, inc=1, device_id=peer(stage, d), device_id_type=MESH)

    loads = [[], []]
    loads[0].append(
        pltpu.make_async_copy(rhs_hbm, rhs.at[pl.ds(ROWS * y, ROWS), :], load_sem.at[8])
    )
    for s in range(2):
        for i, (src, dst) in enumerate(
            ((row_hbm, row), (col_hbm, col), (left_hbm, left), (right_hbm, right))
        ):
            loads[s].append(pltpu.make_async_copy(src.at[s], dst.at[s], load_sem.at[4 * s + i]))
        loads[s].append(
            pltpu.make_async_copy(
                diag_hbm.at[s], inv.at[s, :, pl.ds(SHARE * y, SHARE), :], own_sem.at[s]
            )
        )
    for s in range(2):
        for c in loads[s]:
            c.start()

    lane128 = lax.broadcasted_iota(jnp.int32, (8, LANES), 1)
    slot_of, within = lane128 // RANK, lane128 % RANK
    sub128 = lax.broadcasted_iota(jnp.int32, (8, LANES), 0)
    totals = [jnp.zeros((LOWER, LANES), F32), jnp.zeros((UPPER, LANES), F32)]

    def solve(unit):
        s, m = ORDER[unit]
        rows = LOWER if s == 0 else UPPER
        earlier = list(range(m)) if s == 0 else list(range(m + 1, BLOCKS))
        later = list(range(m + 1, BLOCKS)) if s == 0 else list(range(m))
        if s == 0:
            side = jnp.concatenate([rhs[:, m * WIDTH : (m + 1) * WIDTH], -row[0, m]], axis=0)
        else:
            side = jnp.concatenate([sol0[m], -row[1, m]], axis=0)
        if earlier:
            reduced, tiles = [], []
            for h in sorted({(m ^ k) // PACK for k in earlier}):
                ranks = jnp.zeros((8, LANES), jnp.int32)
                piece = jnp.zeros((rows, LANES), F32)
                for j in range(h * PACK, (h + 1) * PACK):
                    k = m ^ j
                    if k not in earlier:
                        tiles.append(jnp.zeros((RANK, WIDTH), F32))
                        continue
                    p = pair_index(m, k)
                    tiles.append(left[s, p])
                    rank = jnp.where(pattern_ref[s, p] == 1, rank_ref[s, p], 0)
                    hit = slot_of == j - h * PACK
                    ranks = jnp.where(hit, rank, ranks)
                    from_k = red[k, :rows, h * LANES : (h + 1) * LANES]
                    piece = jnp.where(jnp.tile(hit, (rows // 8, 1)), from_k, piece)
                keep = jnp.where(within < ranks, 1.0, 0.0).astype(F32)
                reduced.append(piece * jnp.tile(keep, (rows // 8, 1)))
            reduced = jnp.concatenate(reduced, axis=1)
            side = side - times(reduced, jnp.concatenate(tiles, axis=0), False)
        for d in range(1, RING):
            unit_copy(unit, (home + d) % RING).wait_recv()
        if unit == STRIDE - 1:
            pl.semaphore_wait(barrier, RING - 1 + 2 * (OCTET - 1))
        if unit % STRIDE == STRIDE - 1 and unit + WINDOW - STRIDE < UNITS - 1:
            for d in range(1, RING):
                pl.semaphore_signal(
                    go_sem, inc=1, device_id=(g, (home + d) % RING), device_id_type=MESH
                )
        solved = times(side, inv[s, m], True)
        if s == 0:
            sol0[m] = solved
        else:
            sol1[m] = solved
        tiles = [col[s, m]] + [
            right[s, pair_index(m, m ^ j)] if (m ^ j) in later else jnp.zeros((RANK, WIDTH), F32)
            for j in range(1, BLOCKS)
        ]
        count = BLOCKS if any((m ^ k) >= PACK for k in later) else PACK
        onward = times(solved, jnp.concatenate(tiles[:count], axis=0), True)
        if later:
            red[m, :rows, : count * RANK] = onward
        totals[s] = totals[s] + onward[:, :LANES]

    low_lanes = lane128 < RANK
    low_tall = jnp.tile(low_lanes, (ALL // 8, 1))
    unit_pack = jnp.concatenate(
        [
            jnp.where(lane128 % RANK == sub128 + 8 * (lane128 // RANK), 1.0, 0.0).astype(F32),
            jnp.zeros((VROWS, LANES), F32),
        ],
        axis=0,
    )
    only_v = jnp.concatenate([jnp.zeros((8, LANES), F32), jnp.ones((VROWS, LANES), F32)], axis=0)

    def turned(x, groups):
        groups = groups % PACK
        return pltpu.roll(x, RANK * groups, 1) if groups else x

    def beside(x, group_rows):
        x = jnp.where(low_tall[: x.shape[0]], x, 0.0)
        total = x[:group_rows]
        for i in range(1, PACK):
            total = total + turned(x[group_rows * i : group_rows * (i + 1)], i)
        return total

    def packed(gain_rows, v):
        return jnp.concatenate([unit_pack[:8] + beside(gain_rows, 8), beside(v, VROWS)], axis=0)

    def below(v):
        stacked = jnp.concatenate([turned(v, PACK - i) for i in range(PACK)], axis=0)
        return jnp.where(low_tall, stacked, 0.0)

    def spread(m):
        a = m[:8]
        rolled = [turned(a, i) for i in range(PACK)]
        strips = []
        for b in range(PACK):
            for i in range(PACK):
                strips.append(jnp.where(lane128 // RANK == b, rolled[(b - i) % PACK], 0.0))
        return jnp.concatenate(strips, axis=0)

    def after(first, then):
        return times(first, spread(then), False) + then * only_v

    def map_copy(s, stage, d):
        return pltpu.make_async_remote_copy(
            src_ref=pack.at[s, stage, places[stage]],
            dst_ref=pack.at[s, stage, places[stage]],
            send_sem=map_send.at[s, stage, d - 1],
            recv_sem=map_recv.at[s, stage, d - 1],
            device_id=peer(stage, d),
            device_id_type=MESH,
        )

    def map_arrived(s, stage, d):
        here = pack.at[s, stage, (places[stage] + OCTET - d) % OCTET]
        pltpu.make_async_remote_copy(
            src_ref=here,
            dst_ref=here,
            send_sem=map_send.at[s, stage, d - 1],
            recv_sem=map_recv.at[s, stage, d - 1],
            device_id=peer(stage, d),
            device_id_type=MESH,
        ).wait_recv()

    def send_map(s, stage, one):
        pack[s, stage, places[stage]] = one
        for d in range(1, OCTET):
            map_copy(s, stage, d).start()

    def join_maps(s, stage):
        for d in range(1, OCTET):
            map_arrived(s, stage, d)
        mine = places[stage] if s == 0 else OCTET - 1 - places[stage]
        nodes = [pack[s, stage, i if s == 0 else OCTET - 1 - i] for i in range(OCTET)]
        ahead = None
        while len(nodes) > 1:
            left_one = unit_pack
            size = OCTET // len(nodes)
            for i in range(0, len(nodes), 2):
                left_one = jnp.where(mine // size == i + 1, nodes[i], left_one)
            if len(nodes) > 2 or stage == 0:
                nodes = [after(nodes[i], nodes[i + 1]) for i in range(0, len(nodes), 2)]
            else:
                nodes = nodes[:1]
            ahead = left_one if ahead is None else after(left_one, ahead)
        return nodes[0], ahead

    near, carried = None, None
    for unit in range(UNITS):
        if unit == 0:
            for c in loads[0]:
                c.wait()
            for d in range(1, RING):
                rhs_copy((home + d) % RING).wait_recv()
        if unit == BLOCKS:
            for c in loads[1]:
                c.wait()
        solve(unit)
        if unit == BLOCKS - 1:
            send_map(0, 0, packed(totals[0][ALL:], totals[0][:ALL]))
        if unit == BLOCKS + 2:
            whole, near = join_maps(0, 0)
            send_map(0, 1, whole)
        if unit == BLOCKS + 5:
            carried = below(after(join_maps(0, 1)[1], near)[8:])

    early = turned(carried, ALL // RANK)
    upper_v = totals[1][:ALL] + times(early, totals[1], False)
    send_map(1, 0, packed(totals[1][LOWER:], upper_v))
    for m in range(BLOCKS):
        sol1[m, :ALL, :] = sol1[m, :ALL, :] + times(early, sol1[m], False)
    whole, near = join_maps(1, 0)
    send_map(1, 1, whole)
    entering = below(after(join_maps(1, 1)[1], near)[8:])

    late = turned(entering, LOWER // RANK)
    for part in range(PARTS):
        for m in range(part * BLOCKS // PARTS, (part + 1) * BLOCKS // PARTS):
            result[:, m * WIDTH : (m + 1) * WIDTH] = sol1[m, :ALL, :] + times(
                late, sol1[m], False
            )
        for d in FAR_FIRST:
            out_copy(part, d).start()
    out_ref[...] = result[pl.ds(pl.multiple_of(ROWS * y, ROWS), ROWS), :]

    for s in range(2):
        for stage in range(2):
            for d in range(1, OCTET):
                map_copy(s, stage, d).wait_send()
    for part in range(PARTS):
        for d in range(1, RING):
            out_copy(part, d).wait_send()


def shards(rhs, diag, left, right, rank, pattern, row, col):
    hbm = pl.BlockSpec(memory_space=pl.ANY)
    smem = pl.BlockSpec(memory_space=pltpu.SMEM)
    return pl.pallas_call(
        kernel,
        out_shape=jax.ShapeDtypeStruct(rhs.shape, F32),
        in_specs=[hbm, hbm, hbm, hbm, smem, smem, hbm, hbm],
        out_specs=pl.BlockSpec(memory_space=pltpu.VMEM),
        scratch_shapes=[
            pltpu.VMEM((ALL, rhs.shape[1]), F32),
            pltpu.VMEM((2, BLOCKS, WIDTH, WIDTH), F32),
            pltpu.VMEM(left.shape, F32),
            pltpu.VMEM(right.shape, F32),
            pltpu.VMEM(row.shape, F32),
            pltpu.VMEM(col.shape, F32),
            pltpu.VMEM((BLOCKS, LOWER, WIDTH), F32),
            pltpu.VMEM((BLOCKS, UPPER, WIDTH), F32),
            pltpu.VMEM((BLOCKS, UPPER, WIDTH), F32),
            pltpu.VMEM((2, 2, OCTET, MAP, LANES), F32),
            pltpu.VMEM((ALL, rhs.shape[1]), F32),
            pltpu.SemaphoreType.DMA((9,)),
            pltpu.SemaphoreType.DMA((2,)),
            pltpu.SemaphoreType.DMA((UNITS,)),
            pltpu.SemaphoreType.DMA((UNITS, RING - 1)),
            pltpu.SemaphoreType.DMA,
            pltpu.SemaphoreType.DMA((RING - 1,)),
            pltpu.SemaphoreType.DMA((2, 2, OCTET - 1)),
            pltpu.SemaphoreType.DMA((2, 2, OCTET - 1)),
            pltpu.SemaphoreType.DMA((PARTS, RING - 1)),
            pltpu.SemaphoreType.DMA((PARTS,)),
            pltpu.SemaphoreType.REGULAR,
            pltpu.SemaphoreType.DMA((UNITS,)),
            pltpu.SemaphoreType.DMA((UNITS,)),
        ],
        compiler_params=pltpu.CompilerParams(
            collective_id=0, has_side_effects=True, vmem_limit_bytes=60 * 1024 * 1024
        ),
        cost_estimate=pl.CostEstimate(
            flops=400_000_000, bytes_accessed=6_000_000, transcendentals=0
        ),
    )(rhs, diag, left, right, rank, pattern, row, col)


def solution(mesh):
    return jax.shard_map(
        shards,
        mesh=mesh,
        in_specs=(
            P("rhs", "blk"),
            P(None, "blk", "rhs", None),
            P(None, "blk", None, None),
            P(None, "blk", None, None),
            P(None, "blk"),
            P(None, "blk"),
            P(None, "blk", None, None),
            P(None, "blk", None, None),
        ),
        out_specs=P("rhs", "blk"),
        check_vma=False,
    )
```

```python
import functools

import jax
import jax.numpy as jnp
from jax import lax
from jax.experimental import pallas as pl
from jax.experimental.pallas import tpu as pltpu
from jax.sharding import PartitionSpec as P

F32 = jnp.float32
BF16 = jnp.bfloat16
MESH = pl.DeviceIdType.MESH

WIDTH = 256
RANK = 32
BLOCKS = 8
RING = 8
ROWS = 8
ALL = ROWS * RING
LOWER = ALL + RANK
UPPER = LOWER + RANK
SHARE = WIDTH // RING
OCTET = 8
UNITS = 2 * BLOCKS
LANES = 128
PACK = LANES // RANK
VROWS = ALL // PACK
MAP = 8 + VROWS
FAR_FIRST = (4, 5, 3, 6, 2, 7, 1)
PARTS = 2
WINDOW = 8
RELAYED = (1, 3, 5, 7, 9, 11, 13)
OPPOSITE, BESIDE = RING // 2, RING // 2 - 1
DELAY = 2
STRIDE = 2

ORDER = [(0, m) for m in range(BLOCKS)] + [(1, m) for m in reversed(range(BLOCKS))]


def pair_index(a, b):
    high, low = max(a, b), min(a, b)
    return high * (high - 1) // 2 + low


def parts(x):
    high = x.astype(BF16)
    return high, (x - high.astype(F32)).astype(BF16)


def times(a, b, trans):
    rows = a.shape[0]
    top = a.astype(BF16).astype(F32)
    stacked = jnp.concatenate([top, a - top], axis=0).astype(BF16)
    dims = (((1,), (1 if trans else 0,)), ((), ()))
    high, low = parts(b)
    p = lax.dot_general(stacked, high, dims, preferred_element_type=F32)
    q = lax.dot_general(a.astype(BF16), low, dims, preferred_element_type=F32)
    return p[:rows] + (p[rows:] + q)


def kernel(
    rhs_hbm, diag_hbm, left_hbm, right_hbm, rank_ref, pattern_ref, row_hbm, col_hbm,
    out_ref,
    rhs, inv, left, right, row, col, sol0, sol1, red, pack, result,
    load_sem, own_sem, unit_send, unit_recv, rhs_send, rhs_recv,
    map_send, map_recv, out_send, out_recv, go_sem, relay_send, relay_recv,
):
    g = lax.axis_index("blk")
    y = lax.axis_index("rhs")
    places = (g % OCTET, g // OCTET)
    home = (RING // 2) * (g % 2)
    barrier = pltpu.get_barrier_semaphore()

    def unit_copy(unit, origin):
        s, m = ORDER[unit]
        return pltpu.make_async_remote_copy(
            src_ref=diag_hbm.at[s, m],
            dst_ref=inv.at[s, m, pl.ds(SHARE * origin, SHARE), :],
            send_sem=unit_send.at[unit],
            recv_sem=unit_recv.at[unit, (origin - home + RING) % RING - 1],
            device_id=(g, home),
            device_id_type=MESH,
        )

    far = (home + OPPOSITE) % RING

    def relay_copy(unit, hop):
        s, m = ORDER[unit]
        here = inv.at[s, m, pl.ds(SHARE * far, SHARE), :]
        return pltpu.make_async_remote_copy(
            src_ref=diag_hbm.at[s, m] if hop == 0 else here,
            dst_ref=here,
            send_sem=unit_send.at[unit] if hop == 0 else relay_send.at[unit],
            recv_sem=relay_recv.at[unit] if hop == 0 else unit_recv.at[unit, OPPOSITE - 1],
            device_id=(g, (home + BESIDE) % RING if hop == 0 else home),
            device_id_type=MESH,
        )

    def rhs_copy(origin):
        return pltpu.make_async_remote_copy(
            src_ref=rhs_hbm,
            dst_ref=rhs.at[pl.ds(ROWS * origin, ROWS), :],
            send_sem=rhs_send,
            recv_sem=rhs_recv.at[(origin - home + RING) % RING - 1],
            device_id=(g, home),
            device_id_type=MESH,
        )

    width = out_ref.shape[1] // PARTS

    def out_copy(part, d):
        n = (home + d) % RING
        return pltpu.make_async_remote_copy(
            src_ref=result.at[pl.ds(ROWS * n, ROWS), pl.ds(part * width, width)],
            dst_ref=out_ref.at[:, pl.ds(part * width, width)],
            send_sem=out_send.at[part, d - 1],
            recv_sem=out_recv.at[part],
            device_id=(g, n),
            device_id_type=MESH,
        )

    @pl.when(y != home)
    def _():
        step = (y - home + RING) % RING
        pl.semaphore_signal(barrier, inc=1, device_id=(g, home), device_id_type=MESH)

        @pl.when(step == BESIDE)
        def _():
            pl.semaphore_signal(barrier, inc=1, device_id=(g, far), device_id_type=MESH)

        pl.semaphore_wait(barrier, jnp.where(step == OPPOSITE, 2, 1))
        rhs_copy(y).start()
        for unit in range(UNITS):
            if unit >= WINDOW and unit % STRIDE == 0:
                pl.semaphore_wait(go_sem, 1)
            if unit in RELAYED:

                @pl.when(step == OPPOSITE)
                def _():
                    relay_copy(unit, 0).start()

                @pl.when(step != OPPOSITE)
                def _():
                    unit_copy(unit, y).start()

            else:
                unit_copy(unit, y).start()
            if unit - DELAY in RELAYED:

                @pl.when(step == BESIDE)
                def _():
                    relay_copy(unit - DELAY, 0).wait_recv()
                    relay_copy(unit - DELAY, 1).start()

        rhs_copy(y).wait_send()
        for unit in range(UNITS):
            unit_copy(unit, y).wait_send()

        @pl.when(step == BESIDE)
        def _():
            for unit in RELAYED:
                relay_copy(unit, 1).wait_send()

        for part in range(PARTS):
            out_copy(part, 1).wait_recv()

    @pl.when(y == home)
    def _():
        solve_group(
            g, y, places, home, barrier, unit_copy, rhs_copy, out_copy,
            rhs_hbm, diag_hbm, left_hbm, right_hbm, rank_ref, pattern_ref, row_hbm, col_hbm,
            out_ref,
            rhs, inv, left, right, row, col, sol0, sol1, red, pack, result,
            load_sem, own_sem, map_send, map_recv, go_sem,
        )


def solve_group(
    g, y, places, home, barrier, unit_copy, rhs_copy, out_copy,
    rhs_hbm, diag_hbm, left_hbm, right_hbm, rank_ref, pattern_ref, row_hbm, col_hbm,
    out_ref,
    rhs, inv, left, right, row, col, sol0, sol1, red, pack, result,
    load_sem, own_sem, map_send, map_recv, go_sem,
):
    for d in range(1, RING):
        pl.semaphore_signal(
            barrier, inc=1, device_id=(g, (home + d) % RING), device_id_type=MESH
        )

    def peer(stage, d):
        there = (places[stage] + d) % OCTET
        if stage == 0:
            return (places[1] * OCTET + there, (RING // 2) * (there % 2))
        return (there * OCTET + places[0], home)

    for stage in range(2):
        for d in range(1, OCTET):
            pl.semaphore_signal(barrier, inc=1, device_id=peer(stage, d), device_id_type=MESH)

    loads = [[], []]
    loads[0].append(
        pltpu.make_async_copy(rhs_hbm, rhs.at[pl.ds(ROWS * y, ROWS), :], load_sem.at[8])
    )
    for s in range(2):
        for i, (src, dst) in enumerate(
            ((row_hbm, row), (col_hbm, col), (left_hbm, left), (right_hbm, right))
        ):
            loads[s].append(pltpu.make_async_copy(src.at[s], dst.at[s], load_sem.at[4 * s + i]))
        loads[s].append(
            pltpu.make_async_copy(
                diag_hbm.at[s], inv.at[s, :, pl.ds(SHARE * y, SHARE), :], own_sem.at[s]
            )
        )
    for s in range(2):
        for c in loads[s]:
            c.start()

    lane128 = lax.broadcasted_iota(jnp.int32, (8, LANES), 1)
    slot_of, within = lane128 // RANK, lane128 % RANK
    sub128 = lax.broadcasted_iota(jnp.int32, (8, LANES), 0)
    totals = [jnp.zeros((LOWER, LANES), F32), jnp.zeros((UPPER, LANES), F32)]

    def solve(unit):
        s, m = ORDER[unit]
        rows = LOWER if s == 0 else UPPER
        earlier = list(range(m)) if s == 0 else list(range(m + 1, BLOCKS))
        later = list(range(m + 1, BLOCKS)) if s == 0 else list(range(m))
        if s == 0:
            side = jnp.concatenate([rhs[:, m * WIDTH : (m + 1) * WIDTH], -row[0, m]], axis=0)
        else:
            side = jnp.concatenate([sol0[m], -row[1, m]], axis=0)
        if earlier:
            reduced, tiles = [], []
            for h in sorted({(m ^ k) // PACK for k in earlier}):
                ranks = jnp.zeros((8, LANES), jnp.int32)
                piece = jnp.zeros((rows, LANES), F32)
                for j in range(h * PACK, (h + 1) * PACK):
                    k = m ^ j
                    if k not in earlier:
                        tiles.append(jnp.zeros((RANK, WIDTH), F32))
                        continue
                    p = pair_index(m, k)
                    tiles.append(left[s, p])
                    rank = jnp.where(pattern_ref[s, p] == 1, rank_ref[s, p], 0)
                    hit = slot_of == j - h * PACK
                    ranks = jnp.where(hit, rank, ranks)
                    from_k = red[k, :rows, h * LANES : (h + 1) * LANES]
                    piece = jnp.where(jnp.tile(hit, (rows // 8, 1)), from_k, piece)
                keep = jnp.where(within < ranks, 1.0, 0.0).astype(F32)
                reduced.append(piece * jnp.tile(keep, (rows // 8, 1)))
            reduced = jnp.concatenate(reduced, axis=1)
            side = side - times(reduced, jnp.concatenate(tiles, axis=0), False)
        for d in range(1, RING):
            unit_copy(unit, (home + d) % RING).wait_recv()
        if unit == STRIDE - 1:
            pl.semaphore_wait(barrier, RING - 1 + 2 * (OCTET - 1))
        if unit % STRIDE == STRIDE - 1 and unit + WINDOW - STRIDE < UNITS - 1:
            for d in range(1, RING):
                pl.semaphore_signal(
                    go_sem, inc=1, device_id=(g, (home + d) % RING), device_id_type=MESH
                )
        solved = times(side, inv[s, m], True)
        if s == 0:
            sol0[m] = solved
        else:
            sol1[m] = solved
        tiles = [col[s, m]] + [
            right[s, pair_index(m, m ^ j)] if (m ^ j) in later else jnp.zeros((RANK, WIDTH), F32)
            for j in range(1, BLOCKS)
        ]
        count = BLOCKS if any((m ^ k) >= PACK for k in later) else PACK
        onward = times(solved, jnp.concatenate(tiles[:count], axis=0), True)
        if later:
            red[m, :rows, : count * RANK] = onward
        totals[s] = totals[s] + onward[:, :LANES]

    low_lanes = lane128 < RANK
    low_tall = jnp.tile(low_lanes, (ALL // 8, 1))
    unit_pack = jnp.concatenate(
        [
            jnp.where(lane128 % RANK == sub128 + 8 * (lane128 // RANK), 1.0, 0.0).astype(F32),
            jnp.zeros((VROWS, LANES), F32),
        ],
        axis=0,
    )
    only_v = jnp.concatenate([jnp.zeros((8, LANES), F32), jnp.ones((VROWS, LANES), F32)], axis=0)

    def turned(x, groups):
        groups = groups % PACK
        return pltpu.roll(x, RANK * groups, 1) if groups else x

    def beside(x, group_rows):
        x = jnp.where(low_tall[: x.shape[0]], x, 0.0)
        total = x[:group_rows]
        for i in range(1, PACK):
            total = total + turned(x[group_rows * i : group_rows * (i + 1)], i)
        return total

    def packed(gain_rows, v):
        return jnp.concatenate([unit_pack[:8] + beside(gain_rows, 8), beside(v, VROWS)], axis=0)

    def below(v):
        stacked = jnp.concatenate([turned(v, PACK - i) for i in range(PACK)], axis=0)
        return jnp.where(low_tall, stacked, 0.0)

    def spread(m):
        a = m[:8]
        rolled = [turned(a, i) for i in range(PACK)]
        strips = []
        for b in range(PACK):
            for i in range(PACK):
                strips.append(jnp.where(lane128 // RANK == b, rolled[(b - i) % PACK], 0.0))
        return jnp.concatenate(strips, axis=0)

    def after(first, then):
        return times(first, spread(then), False) + then * only_v

    def map_copy(s, stage, d):
        return pltpu.make_async_remote_copy(
            src_ref=pack.at[s, stage, places[stage]],
            dst_ref=pack.at[s, stage, places[stage]],
            send_sem=map_send.at[s, stage, d - 1],
            recv_sem=map_recv.at[s, stage, d - 1],
            device_id=peer(stage, d),
            device_id_type=MESH,
        )

    def map_arrived(s, stage, d):
        here = pack.at[s, stage, (places[stage] + OCTET - d) % OCTET]
        pltpu.make_async_remote_copy(
            src_ref=here,
            dst_ref=here,
            send_sem=map_send.at[s, stage, d - 1],
            recv_sem=map_recv.at[s, stage, d - 1],
            device_id=peer(stage, d),
            device_id_type=MESH,
        ).wait_recv()

    def send_map(s, stage, one):
        pack[s, stage, places[stage]] = one
        for d in range(1, OCTET):
            map_copy(s, stage, d).start()

    def join_maps(s, stage):
        for d in range(1, OCTET):
            map_arrived(s, stage, d)
        mine = places[stage] if s == 0 else OCTET - 1 - places[stage]
        nodes = [pack[s, stage, i if s == 0 else OCTET - 1 - i] for i in range(OCTET)]
        ahead = None
        while len(nodes) > 1:
            left_one = unit_pack
            size = OCTET // len(nodes)
            for i in range(0, len(nodes), 2):
                left_one = jnp.where(mine // size == i + 1, nodes[i], left_one)
            if len(nodes) > 2 or stage == 0:
                nodes = [after(nodes[i], nodes[i + 1]) for i in range(0, len(nodes), 2)]
            else:
                nodes = nodes[:1]
            ahead = left_one if ahead is None else after(left_one, ahead)
        return nodes[0], ahead

    near, carried = None, None
    for unit in range(UNITS):
        if unit == 0:
            for c in loads[0]:
                c.wait()
            for d in range(1, RING):
                rhs_copy((home + d) % RING).wait_recv()
        if unit == BLOCKS:
            for c in loads[1]:
                c.wait()
        solve(unit)
        if unit == BLOCKS - 1:
            send_map(0, 0, packed(totals[0][ALL:], totals[0][:ALL]))
        if unit == BLOCKS + 2:
            whole, near = join_maps(0, 0)
            send_map(0, 1, whole)
        if unit == BLOCKS + 5:
            carried = below(after(join_maps(0, 1)[1], near)[8:])

    early = turned(carried, ALL // RANK)
    upper_v = totals[1][:ALL] + times(early, totals[1], False)
    send_map(1, 0, packed(totals[1][LOWER:], upper_v))
    for m in range(BLOCKS):
        sol1[m, :ALL, :] = sol1[m, :ALL, :] + times(early, sol1[m], False)
    whole, near = join_maps(1, 0)
    send_map(1, 1, whole)
    entering = below(after(join_maps(1, 1)[1], near)[8:])

    late = turned(entering, LOWER // RANK)
    for part in range(PARTS):
        for m in range(part * BLOCKS // PARTS, (part + 1) * BLOCKS // PARTS):
            result[:, m * WIDTH : (m + 1) * WIDTH] = sol1[m, :ALL, :] + times(
                late, sol1[m], False
            )
        for d in FAR_FIRST:
            out_copy(part, d).start()
    out_ref[...] = result[pl.ds(pl.multiple_of(ROWS * y, ROWS), ROWS), :]

    for s in range(2):
        for stage in range(2):
            for d in range(1, OCTET):
                map_copy(s, stage, d).wait_send()
    for part in range(PARTS):
        for d in range(1, RING):
            out_copy(part, d).wait_send()


def shards(rhs, diag, left, right, rank, pattern, row, col):
    hbm = pl.BlockSpec(memory_space=pl.ANY)
    smem = pl.BlockSpec(memory_space=pltpu.SMEM)
    return pl.pallas_call(
        kernel,
        out_shape=jax.ShapeDtypeStruct(rhs.shape, F32),
        in_specs=[hbm, hbm, hbm, hbm, smem, smem, hbm, hbm],
        out_specs=pl.BlockSpec(memory_space=pltpu.VMEM),
        scratch_shapes=[
            pltpu.VMEM((ALL, rhs.shape[1]), F32),
            pltpu.VMEM((2, BLOCKS, WIDTH, WIDTH), F32),
            pltpu.VMEM(left.shape, F32),
            pltpu.VMEM(right.shape, F32),
            pltpu.VMEM(row.shape, F32),
            pltpu.VMEM(col.shape, F32),
            pltpu.VMEM((BLOCKS, LOWER, WIDTH), F32),
            pltpu.VMEM((BLOCKS, UPPER, WIDTH), F32),
            pltpu.VMEM((BLOCKS, UPPER, WIDTH), F32),
            pltpu.VMEM((2, 2, OCTET, MAP, LANES), F32),
            pltpu.VMEM((ALL, rhs.shape[1]), F32),
            pltpu.SemaphoreType.DMA((9,)),
            pltpu.SemaphoreType.DMA((2,)),
            pltpu.SemaphoreType.DMA((UNITS,)),
            pltpu.SemaphoreType.DMA((UNITS, RING - 1)),
            pltpu.SemaphoreType.DMA,
            pltpu.SemaphoreType.DMA((RING - 1,)),
            pltpu.SemaphoreType.DMA((2, 2, OCTET - 1)),
            pltpu.SemaphoreType.DMA((2, 2, OCTET - 1)),
            pltpu.SemaphoreType.DMA((PARTS, RING - 1)),
            pltpu.SemaphoreType.DMA((PARTS,)),
            pltpu.SemaphoreType.REGULAR,
            pltpu.SemaphoreType.DMA((UNITS,)),
            pltpu.SemaphoreType.DMA((UNITS,)),
        ],
        compiler_params=pltpu.CompilerParams(
            collective_id=0, has_side_effects=True, vmem_limit_bytes=60 * 1024 * 1024
        ),
        cost_estimate=pl.CostEstimate(
            flops=400_000_000, bytes_accessed=6_000_000, transcendentals=0
        ),
    )(rhs, diag, left, right, rank, pattern, row, col)


def solution(mesh):
    return jax.shard_map(
        shards,
        mesh=mesh,
        in_specs=(
            P("rhs", "blk"),
            P(None, "blk", "rhs", None),
            P(None, "blk", None, None),
            P(None, "blk", None, None),
            P(None, "blk"),
            P(None, "blk"),
            P(None, "blk", None, None),
            P(None, "blk", None, None),
        ),
        out_specs=P("rhs", "blk"),
        check_vma=False,
    )
```

```python
import functools

import jax
import jax.numpy as jnp
from jax import lax
from jax.experimental import pallas as pl
from jax.experimental.pallas import tpu as pltpu
from jax.sharding import PartitionSpec as P

F32 = jnp.float32
BF16 = jnp.bfloat16
MESH = pl.DeviceIdType.MESH

WIDTH = 256
RANK = 32
BLOCKS = 8
RING = 8
ROWS = 8
ALL = ROWS * RING
LOWER = ALL + RANK
UPPER = LOWER + RANK
SHARE = WIDTH // RING
OCTET = 8
UNITS = 2 * BLOCKS
LANES = 128
PACK = LANES // RANK
VROWS = ALL // PACK
MAP = 8 + VROWS
FAR_FIRST = (4, 5, 3, 6, 2, 7, 1)
PARTS = 2
WINDOW = 8
RELAYED = (1, 3, 5, 7, 9, 11, 13)
OPPOSITE, BESIDE = RING // 2, RING // 2 - 1
DELAY = 2
STRIDE = 2

ORDER = [(0, m) for m in range(BLOCKS)] + [(1, m) for m in reversed(range(BLOCKS))]


def pair_index(a, b):
    high, low = max(a, b), min(a, b)
    return high * (high - 1) // 2 + low


def parts(x):
    high = x.astype(BF16)
    return high, (x - high.astype(F32)).astype(BF16)


def times(a, b, trans):
    rows = a.shape[0]
    top = a.astype(BF16).astype(F32)
    stacked = jnp.concatenate([top, a - top], axis=0).astype(BF16)
    dims = (((1,), (1 if trans else 0,)), ((), ()))
    high, low = parts(b)
    p = lax.dot_general(stacked, high, dims, preferred_element_type=F32)
    q = lax.dot_general(a.astype(BF16), low, dims, preferred_element_type=F32)
    return p[:rows] + (p[rows:] + q)


def kernel(
    rhs_hbm, diag_hbm, left_hbm, right_hbm, rank_ref, pattern_ref, row_hbm, col_hbm,
    out_ref,
    rhs, inv, left, right, row, col, sol0, sol1, red, pack, result,
    load_sem, own_sem, unit_send, unit_recv, rhs_send, rhs_recv,
    map_send, map_recv, out_send, out_recv, go_sem, relay_send, relay_recv,
):
    g = lax.axis_index("blk")
    y = lax.axis_index("rhs")
    places = (g % OCTET, g // OCTET)
    home = (RING // 2) * (g % 2)
    barrier = pltpu.get_barrier_semaphore()

    def unit_copy(unit, origin):
        s, m = ORDER[unit]
        return pltpu.make_async_remote_copy(
            src_ref=diag_hbm.at[s, m],
            dst_ref=inv.at[s, m, pl.ds(SHARE * origin, SHARE), :],
            send_sem=unit_send.at[unit],
            recv_sem=unit_recv.at[unit, (origin - home + RING) % RING - 1],
            device_id=(g, home),
            device_id_type=MESH,
        )

    far = (home + OPPOSITE) % RING

    def relay_copy(unit, hop):
        s, m = ORDER[unit]
        here = inv.at[s, m, pl.ds(SHARE * far, SHARE), :]
        return pltpu.make_async_remote_copy(
            src_ref=diag_hbm.at[s, m] if hop == 0 else here,
            dst_ref=here,
            send_sem=unit_send.at[unit] if hop == 0 else relay_send.at[unit],
            recv_sem=relay_recv.at[unit] if hop == 0 else unit_recv.at[unit, OPPOSITE - 1],
            device_id=(g, (home + BESIDE) % RING if hop == 0 else home),
            device_id_type=MESH,
        )

    def rhs_copy(origin):
        return pltpu.make_async_remote_copy(
            src_ref=rhs_hbm,
            dst_ref=rhs.at[pl.ds(ROWS * origin, ROWS), :],
            send_sem=rhs_send,
            recv_sem=rhs_recv.at[(origin - home + RING) % RING - 1],
            device_id=(g, home),
            device_id_type=MESH,
        )

    width = out_ref.shape[1] // PARTS

    def out_copy(part, d):
        n = (home + d) % RING
        return pltpu.make_async_remote_copy(
            src_ref=result.at[pl.ds(ROWS * n, ROWS), pl.ds(part * width, width)],
            dst_ref=out_ref.at[:, pl.ds(part * width, width)],
            send_sem=out_send.at[part, d - 1],
            recv_sem=out_recv.at[part],
            device_id=(g, n),
            device_id_type=MESH,
        )

    @pl.when(y != home)
    def _():
        step = (y - home + RING) % RING
        pl.semaphore_signal(barrier, inc=1, device_id=(g, home), device_id_type=MESH)

        @pl.when(step == BESIDE)
        def _():
            pl.semaphore_signal(barrier, inc=1, device_id=(g, far), device_id_type=MESH)

        pl.semaphore_wait(barrier, jnp.where(step == OPPOSITE, 2, 1))
        rhs_copy(y).start()
        for unit in range(UNITS):
            if unit >= WINDOW and unit % STRIDE == 0:
                pl.semaphore_wait(go_sem, 1)
            if unit in RELAYED:

                @pl.when(step == OPPOSITE)
                def _():
                    relay_copy(unit, 0).start()

                @pl.when(step != OPPOSITE)
                def _():
                    unit_copy(unit, y).start()

            else:
                unit_copy(unit, y).start()
            if unit - DELAY in RELAYED:

                @pl.when(step == BESIDE)
                def _():
                    relay_copy(unit - DELAY, 0).wait_recv()
                    relay_copy(unit - DELAY, 1).start()

        rhs_copy(y).wait_send()
        for unit in range(UNITS):
            unit_copy(unit, y).wait_send()

        @pl.when(step == BESIDE)
        def _():
            for unit in RELAYED:
                relay_copy(unit, 1).wait_send()

        for part in range(PARTS):
            out_copy(part, 1).wait_recv()

    @pl.when(y == home)
    def _():
        solve_group(
            g, y, places, home, barrier, unit_copy, rhs_copy, out_copy,
            rhs_hbm, diag_hbm, left_hbm, right_hbm, rank_ref, pattern_ref, row_hbm, col_hbm,
            out_ref,
            rhs, inv, left, right, row, col, sol0, sol1, red, pack, result,
            load_sem, own_sem, map_send, map_recv, go_sem,
        )


def solve_group(
    g, y, places, home, barrier, unit_copy, rhs_copy, out_copy,
    rhs_hbm, diag_hbm, left_hbm, right_hbm, rank_ref, pattern_ref, row_hbm, col_hbm,
    out_ref,
    rhs, inv, left, right, row, col, sol0, sol1, red, pack, result,
    load_sem, own_sem, map_send, map_recv, go_sem,
):
    for d in range(1, RING):
        pl.semaphore_signal(
            barrier, inc=1, device_id=(g, (home + d) % RING), device_id_type=MESH
        )

    def peer(stage, d):
        there = (places[stage] + d) % OCTET
        if stage == 0:
            return (places[1] * OCTET + there, (RING // 2) * (there % 2))
        return (there * OCTET + places[0], home)

    for stage in range(2):
        for d in range(1, OCTET):
            pl.semaphore_signal(barrier, inc=1, device_id=peer(stage, d), device_id_type=MESH)

    loads = [[], []]
    loads[0].append(
        pltpu.make_async_copy(rhs_hbm, rhs.at[pl.ds(ROWS * y, ROWS), :], load_sem.at[8])
    )
    for s in range(2):
        for i, (src, dst) in enumerate(
            ((row_hbm, row), (col_hbm, col), (left_hbm, left), (right_hbm, right))
        ):
            loads[s].append(pltpu.make_async_copy(src.at[s], dst.at[s], load_sem.at[4 * s + i]))
        loads[s].append(
            pltpu.make_async_copy(
                diag_hbm.at[s], inv.at[s, :, pl.ds(SHARE * y, SHARE), :], own_sem.at[s]
            )
        )
    for s in range(2):
        for c in loads[s]:
            c.start()

    lane128 = lax.broadcasted_iota(jnp.int32, (8, LANES), 1)
    slot_of, within = lane128 // RANK, lane128 % RANK
    sub128 = lax.broadcasted_iota(jnp.int32, (8, LANES), 0)
    totals = [jnp.zeros((LOWER, LANES), F32), jnp.zeros((UPPER, LANES), F32)]

    def solve(unit):
        s, m = ORDER[unit]
        rows = LOWER if s == 0 else UPPER
        earlier = list(range(m)) if s == 0 else list(range(m + 1, BLOCKS))
        later = list(range(m + 1, BLOCKS)) if s == 0 else list(range(m))
        if s == 0:
            side = jnp.concatenate([rhs[:, m * WIDTH : (m + 1) * WIDTH], -row[0, m]], axis=0)
        else:
            side = jnp.concatenate([sol0[m], -row[1, m]], axis=0)
        if earlier:
            reduced, tiles = [], []
            for h in sorted({(m ^ k) // PACK for k in earlier}):
                ranks = jnp.zeros((8, LANES), jnp.int32)
                piece = jnp.zeros((rows, LANES), F32)
                for j in range(h * PACK, (h + 1) * PACK):
                    k = m ^ j
                    if k not in earlier:
                        tiles.append(jnp.zeros((RANK, WIDTH), F32))
                        continue
                    p = pair_index(m, k)
                    tiles.append(left[s, p])
                    rank = jnp.where(pattern_ref[s, p] == 1, rank_ref[s, p], 0)
                    hit = slot_of == j - h * PACK
                    ranks = jnp.where(hit, rank, ranks)
                    from_k = red[k, :rows, h * LANES : (h + 1) * LANES]
                    piece = jnp.where(jnp.tile(hit, (rows // 8, 1)), from_k, piece)
                keep = jnp.where(within < ranks, 1.0, 0.0).astype(F32)
                reduced.append(piece * jnp.tile(keep, (rows // 8, 1)))
            reduced = jnp.concatenate(reduced, axis=1)
            side = side - times(reduced, jnp.concatenate(tiles, axis=0), False)
        if unit == UNITS - 1:
            early = turned(carried, ALL // RANK)
            side = jnp.concatenate([side[:ALL] + times(early, side, False), side[ALL:]], axis=0)
            totals[s] = jnp.concatenate(
                [totals[s][:ALL] + times(early, totals[s], False), totals[s][ALL:]], axis=0
            )
        for d in range(1, RING):
            unit_copy(unit, (home + d) % RING).wait_recv()
        if unit == STRIDE - 1:
            pl.semaphore_wait(barrier, RING - 1 + 2 * (OCTET - 1))
        if unit % STRIDE == STRIDE - 1 and unit + WINDOW - STRIDE < UNITS - 1:
            for d in range(1, RING):
                pl.semaphore_signal(
                    go_sem, inc=1, device_id=(g, (home + d) % RING), device_id_type=MESH
                )
        solved = times(side, inv[s, m], True)
        if s == 0:
            sol0[m] = solved
        else:
            sol1[m] = solved
        tiles = [col[s, m]] + [
            right[s, pair_index(m, m ^ j)] if (m ^ j) in later else jnp.zeros((RANK, WIDTH), F32)
            for j in range(1, BLOCKS)
        ]
        count = BLOCKS if any((m ^ k) >= PACK for k in later) else PACK
        onward = times(solved, jnp.concatenate(tiles[:count], axis=0), True)
        if later:
            red[m, :rows, : count * RANK] = onward
        totals[s] = totals[s] + onward[:, :LANES]

    low_lanes = lane128 < RANK
    low_tall = jnp.tile(low_lanes, (ALL // 8, 1))
    unit_pack = jnp.concatenate(
        [
            jnp.where(lane128 % RANK == sub128 + 8 * (lane128 // RANK), 1.0, 0.0).astype(F32),
            jnp.zeros((VROWS, LANES), F32),
        ],
        axis=0,
    )
    only_v = jnp.concatenate([jnp.zeros((8, LANES), F32), jnp.ones((VROWS, LANES), F32)], axis=0)

    def turned(x, groups):
        groups = groups % PACK
        return pltpu.roll(x, RANK * groups, 1) if groups else x

    def beside(x, group_rows):
        x = jnp.where(low_tall[: x.shape[0]], x, 0.0)
        total = x[:group_rows]
        for i in range(1, PACK):
            total = total + turned(x[group_rows * i : group_rows * (i + 1)], i)
        return total

    def packed(gain_rows, v):
        return jnp.concatenate([unit_pack[:8] + beside(gain_rows, 8), beside(v, VROWS)], axis=0)

    def below(v):
        stacked = jnp.concatenate([turned(v, PACK - i) for i in range(PACK)], axis=0)
        return jnp.where(low_tall, stacked, 0.0)

    def spread(m):
        a = m[:8]
        rolled = [turned(a, i) for i in range(PACK)]
        strips = []
        for b in range(PACK):
            for i in range(PACK):
                strips.append(jnp.where(lane128 // RANK == b, rolled[(b - i) % PACK], 0.0))
        return jnp.concatenate(strips, axis=0)

    def after(first, then):
        return times(first, spread(then), False) + then * only_v

    def map_copy(s, stage, d):
        return pltpu.make_async_remote_copy(
            src_ref=pack.at[s, stage, places[stage]],
            dst_ref=pack.at[s, stage, places[stage]],
            send_sem=map_send.at[s, stage, d - 1],
            recv_sem=map_recv.at[s, stage, d - 1],
            device_id=peer(stage, d),
            device_id_type=MESH,
        )

    def map_arrived(s, stage, d):
        here = pack.at[s, stage, (places[stage] + OCTET - d) % OCTET]
        pltpu.make_async_remote_copy(
            src_ref=here,
            dst_ref=here,
            send_sem=map_send.at[s, stage, d - 1],
            recv_sem=map_recv.at[s, stage, d - 1],
            device_id=peer(stage, d),
            device_id_type=MESH,
        ).wait_recv()

    def send_map(s, stage, one):
        pack[s, stage, places[stage]] = one
        for d in FAR_FIRST:
            map_copy(s, stage, d).start()

    def join_maps(s, stage):
        for d in range(1, OCTET):
            map_arrived(s, stage, d)
        mine = places[stage] if s == 0 else OCTET - 1 - places[stage]
        nodes = [pack[s, stage, i if s == 0 else OCTET - 1 - i] for i in range(OCTET)]
        ahead = None
        while len(nodes) > 1:
            left_one = unit_pack
            size = OCTET // len(nodes)
            for i in range(0, len(nodes), 2):
                left_one = jnp.where(mine // size == i + 1, nodes[i], left_one)
            if len(nodes) > 2 or stage == 0:
                nodes = [after(nodes[i], nodes[i + 1]) for i in range(0, len(nodes), 2)]
            else:
                nodes = nodes[:1]
            ahead = left_one if ahead is None else after(left_one, ahead)
        return nodes[0], ahead

    near, carried = None, None
    for unit in range(UNITS):
        if unit == 0:
            for c in loads[0]:
                c.wait()
            for d in range(1, RING):
                rhs_copy((home + d) % RING).wait_recv()
        if unit == BLOCKS:
            for c in loads[1]:
                c.wait()
        solve(unit)
        if unit == BLOCKS - 1:
            send_map(0, 0, packed(totals[0][ALL:], totals[0][:ALL]))
        if unit == BLOCKS + 2:
            whole, near = join_maps(0, 0)
            send_map(0, 1, whole)
        if unit == BLOCKS + 5:
            carried = below(after(join_maps(0, 1)[1], near)[8:])

    send_map(1, 0, packed(totals[1][LOWER:], totals[1][:ALL]))
    early = turned(carried, ALL // RANK)
    for m in range(1, BLOCKS):
        sol1[m, :ALL, :] = sol1[m, :ALL, :] + times(early, sol1[m], False)
    whole, near = join_maps(1, 0)
    send_map(1, 1, whole)
    wide = spread(near)
    entering = below(times(join_maps(1, 1)[1][8:], wide, False) + near[8:])

    late = turned(entering, LOWER // RANK)
    for part in range(PARTS):
        for m in range(part * BLOCKS // PARTS, (part + 1) * BLOCKS // PARTS):
            result[:, m * WIDTH : (m + 1) * WIDTH] = sol1[m, :ALL, :] + times(
                late, sol1[m], False
            )
        for d in FAR_FIRST:
            out_copy(part, d).start()
    out_ref[...] = result[pl.ds(pl.multiple_of(ROWS * y, ROWS), ROWS), :]

    for s in range(2):
        for stage in range(2):
            for d in range(1, OCTET):
                map_copy(s, stage, d).wait_send()
    for part in range(PARTS):
        for d in range(1, RING):
            out_copy(part, d).wait_send()


def shards(rhs, diag, left, right, rank, pattern, row, col):
    hbm = pl.BlockSpec(memory_space=pl.ANY)
    smem = pl.BlockSpec(memory_space=pltpu.SMEM)
    return pl.pallas_call(
        kernel,
        out_shape=jax.ShapeDtypeStruct(rhs.shape, F32),
        in_specs=[hbm, hbm, hbm, hbm, smem, smem, hbm, hbm],
        out_specs=pl.BlockSpec(memory_space=pltpu.VMEM),
        scratch_shapes=[
            pltpu.VMEM((ALL, rhs.shape[1]), F32),
            pltpu.VMEM((2, BLOCKS, WIDTH, WIDTH), F32),
            pltpu.VMEM(left.shape, F32),
            pltpu.VMEM(right.shape, F32),
            pltpu.VMEM(row.shape, F32),
            pltpu.VMEM(col.shape, F32),
            pltpu.VMEM((BLOCKS, LOWER, WIDTH), F32),
            pltpu.VMEM((BLOCKS, UPPER, WIDTH), F32),
            pltpu.VMEM((BLOCKS, UPPER, WIDTH), F32),
            pltpu.VMEM((2, 2, OCTET, MAP, LANES), F32),
            pltpu.VMEM((ALL, rhs.shape[1]), F32),
            pltpu.SemaphoreType.DMA((9,)),
            pltpu.SemaphoreType.DMA((2,)),
            pltpu.SemaphoreType.DMA((UNITS,)),
            pltpu.SemaphoreType.DMA((UNITS, RING - 1)),
            pltpu.SemaphoreType.DMA,
            pltpu.SemaphoreType.DMA((RING - 1,)),
            pltpu.SemaphoreType.DMA((2, 2, OCTET - 1)),
            pltpu.SemaphoreType.DMA((2, 2, OCTET - 1)),
            pltpu.SemaphoreType.DMA((PARTS, RING - 1)),
            pltpu.SemaphoreType.DMA((PARTS,)),
            pltpu.SemaphoreType.REGULAR,
            pltpu.SemaphoreType.DMA((UNITS,)),
            pltpu.SemaphoreType.DMA((UNITS,)),
        ],
        compiler_params=pltpu.CompilerParams(
            collective_id=0, has_side_effects=True, vmem_limit_bytes=60 * 1024 * 1024
        ),
        cost_estimate=pl.CostEstimate(
            flops=400_000_000, bytes_accessed=6_000_000, transcendentals=0
        ),
    )(rhs, diag, left, right, rank, pattern, row, col)


def solution(mesh):
    return jax.shard_map(
        shards,
        mesh=mesh,
        in_specs=(
            P("rhs", "blk"),
            P(None, "blk", "rhs", None),
            P(None, "blk", None, None),
            P(None, "blk", None, None),
            P(None, "blk"),
            P(None, "blk"),
            P(None, "blk", None, None),
            P(None, "blk", None, None),
        ),
        out_specs=P("rhs", "blk"),
        check_vma=False,
    )
```
